256 devices in a mesh: query: 8 (over x, y_hi), lib: 32 (over z, y_lo, core).
Axes of the slice: x: 4, y: 4 (y_hi: 2, y_lo: 2; y = y_hi * 2 + y_lo), z: 8, core: 2. Of those that a mesh axis runs over, the one named last changes fastest.
Arguments:
- query_words: int32 [1024, 64], P(('query', 'lib')), may hold values from -2147483648 to 2147483647, as said below
- lib_bits: bfloat16 [262144, 2048], P('lib'), may hold values from 0 to 1, as said below
- cutoff: float32 [262144], P('lib'), may hold values from 0.05 to 0.35
- counts: int32 [512], P('lib'), may hold values from 1 to 8, as said below
- targets: int32 [512, 8], P('lib'), may hold values from 0 to 63
- activity_tiles: bfloat16 [512, 8, 512, 128], P('lib'), may hold values from 0 to 1
Outputs:
- centered_scores: float32 [8192, 1024], P('lib', 'query')
The draws below stay inside these ranges and needn't reach their ends.
Inputs may be any that keep to these rules, and one draw needn't show every extreme that they name: `query_words`: bit k of word w (bit 31 the sign bit, two's complement) is fingerprint bit 32 w + k; some queries have no bit set. `lib_bits`: entries are 0 or 1; some library compounds have no bit set. `counts`: some library block has all 8 slots live.
All inputs are finite; a program needn't handle non-finite values.
Results may differ from the reference program's by a relative error of at most 0.0003.
Values sent between devices are 32-bit elements; how exact they have to be, the bound alone decides.
A program may use at most 192 MiB of HBM per device.

```python
import jax
import jax.numpy as jnp
from jax import lax

NBITS = 2048
NT = 8192
TBLK = 128
BLOCK = 512
KMAX = 8
WORDS = 64
NBLK = 512
NL = 262144
NQ = 1024


scaffold_total = 64


pick_count = 8


def shared_scaffolds(key):
    common = jax.random.fold_in(key, 5)
    key_bits, key_density = jax.random.split(common, 2)
    density = jax.random.randint(key_density, (scaffold_total, 1), 10, 35, dtype=jnp.int32)
    table = jax.random.randint(key_bits, (scaffold_total, NBITS), 0, 1000, dtype=jnp.int32)
    return (table < density).astype(jnp.int32)


def compose(scaffolds, picks):
    return jnp.max(jnp.take(scaffolds, picks, axis=0), axis=-2)


def draw_query_words(key, part):
    scaffolds = shared_scaffolds(key)
    own_key = jax.random.fold_in(key, 11)
    key_one, key_three, key_four, key_five = jax.random.split(own_key, 4)
    picks = jax.random.randint(key_one, (NQ, pick_count), 0, scaffold_total, dtype=jnp.int32)
    rows = compose(scaffolds, picks)
    table = jax.random.randint(key_three, (NQ, NBITS), 0, 1000, dtype=jnp.int32)
    bits = jnp.where(rows == 1, table < 900, table < 10).astype(jnp.int32)
    positions = jnp.arange(NQ, dtype=jnp.int32)
    forced = jax.random.randint(key_five, (), 0, NQ, dtype=jnp.int32)
    empty = (jax.random.randint(key_four, (NQ,), 0, 16, dtype=jnp.int32) == 0) | (positions == forced)
    bits = jnp.where(empty[:, None], 0, bits)
    shifts = jnp.arange(32, dtype=jnp.int32)
    shifted = jnp.left_shift(bits.reshape(NQ, WORDS, 32), shifts[None, None, :])
    return jnp.sum(shifted, axis=2, dtype=jnp.int32)


def draw_lib_bits(key, part):
    scaffolds = shared_scaffolds(key)
    own_key = jax.random.fold_in(key, 23)
    key_flag, key_place, key_forced, key_blocks = jax.random.split(own_key, 4)
    keep_lo = 850
    keep_hi = 950
    added_hi = 30
    flagged = jax.random.randint(key_flag, (NBLK,), 0, 4, dtype=jnp.int32) == 0
    place = jax.random.randint(key_place, (NBLK,), 0, BLOCK, dtype=jnp.int32)
    forced = jax.random.randint(key_forced, (), 0, NBLK, dtype=jnp.int32)
    row_index = jnp.arange(BLOCK, dtype=jnp.int32)

    def one_block(block_index):
        block_key = jax.random.fold_in(key_blocks, block_index)
        key_one, key_two, key_three, key_four = jax.random.split(block_key, 4)
        picks = jax.random.randint(key_one, (BLOCK, pick_count), 0, scaffold_total, dtype=jnp.int32)
        rows = compose(scaffolds, picks)
        keep = jax.random.randint(key_two, (BLOCK, 1), keep_lo, keep_hi, dtype=jnp.int32)
        added = jax.random.randint(key_three, (BLOCK, 1), 5, added_hi, dtype=jnp.int32)
        table = jax.random.randint(key_four, (BLOCK, NBITS), 0, 1000, dtype=jnp.int32)
        bits = jnp.where(rows == 1, table < keep, table < added)
        is_empty = flagged[block_index] | (block_index == forced)
        empty_row = jnp.where(is_empty, place[block_index], -1)
        bits = jnp.where((row_index == empty_row)[:, None], False, bits)
        return bits.astype(jnp.float32).astype(jnp.bfloat16)
    blocks = lax.map(one_block, jnp.arange(NBLK, dtype=jnp.int32))
    return blocks.reshape(NL, NBITS)


def draw_counts(key, part):
    key_one, key_two, key_three = jax.random.split(jax.random.fold_in(key, 37), 3)
    heavy = jax.random.randint(key_one, (NBLK,), 0, 4, dtype=jnp.int32) == 0
    light = jax.random.randint(key_two, (NBLK,), 1, KMAX // 2 + 1, dtype=jnp.int32)
    filled = jnp.where(heavy, KMAX, light)
    position = jax.random.randint(key_three, (), 0, NBLK, dtype=jnp.int32)
    return jnp.where(jnp.arange(NBLK, dtype=jnp.int32) == position, KMAX, filled).astype(jnp.int32)


def draw_targets(key, part):
    return jax.random.randint(jax.random.fold_in(key, 41), (NBLK, KMAX), 0, NT // TBLK, dtype=jnp.int32)


def levels(rng, dims, cuts, least, high):
    factor_of, own = 1.0, jax.random.fold_in(rng, 6)
    for axis_at, blocks in cuts:
        steps = jnp.exp(jax.random.uniform(jax.random.fold_in(own, axis_at), (blocks,), jnp.float32, least / len(cuts), high / len(cuts)))
        factor_of = factor_of * jnp.repeat(steps, dims[axis_at] // blocks).reshape([-1 if axis == axis_at else 1 for axis in range(len(dims))])
    return factor_of


def setup_inputs(seed: int = 0) -> dict:
    key_list = jax.random.split(jax.random.key(seed), 7)
    return {
        "query_words": draw_query_words(jax.random.fold_in(key_list[6], 71), 0),
        "lib_bits": draw_lib_bits(jax.random.fold_in(key_list[6], 71), 0),
        "cutoff": jnp.clip(0.05 + 0.29999999 * jax.random.uniform(key_list[2], (NL,), jnp.float32) ** levels(key_list[2], (NL,), ((0, 32),), -0.2, 0.2), 0.05, 0.35),
        "counts": draw_counts(jax.random.fold_in(key_list[6], 71), 0),
        "targets": draw_targets(jax.random.fold_in(key_list[6], 71), 0),
        "activity_tiles": jnp.clip(1.0 * jax.random.uniform(key_list[5], (NBLK, KMAX, BLOCK, TBLK), jnp.float32) ** levels(key_list[5], (NBLK, KMAX, BLOCK, TBLK), ((0, 32),), -0.2, 0.2), 0.0, 1.0).astype(jnp.bfloat16),
    }


alpha_weight = 0.7
beta_weight = 0.3
steepness = 16.0


def unpack(words):
    shifts = jnp.arange(32, dtype=jnp.int32)
    bit_table = jnp.right_shift(words[:, :, None], shifts[None, None, :]) & 1
    return bit_table.reshape(words.shape[0], words.shape[1] * 32).astype(jnp.bfloat16)


def reference(query_words, lib_bits, cutoff, counts, targets, activity_tiles):
    query_bits = unpack(query_words)
    query_float = query_bits.astype(jnp.float32)
    query_count = jnp.sum(query_float, axis=1)
    inverse_block = 1.0 / BLOCK

    def advance(raw_scores, block_index):
        lib_rows = lax.dynamic_slice_in_dim(lib_bits, block_index * BLOCK, BLOCK, 0).astype(jnp.float32)
        cutoffs = lax.dynamic_slice_in_dim(cutoff, block_index * BLOCK, BLOCK, 0)
        library_count = jnp.sum(lib_rows, axis=1)
        intersection = jnp.dot(lib_rows, query_float.T, precision=lax.Precision.HIGHEST)
        denominator = jnp.maximum(alpha_weight * query_count[None, :] + beta_weight * library_count[:, None], 1.0)
        similarity = intersection / denominator
        soft_hits = jax.nn.sigmoid(steepness * (similarity - cutoffs[:, None])).astype(jnp.bfloat16)
        hits_float = soft_hits.astype(jnp.float32)
        for slot_index in range(KMAX):
            tile = activity_tiles[block_index, slot_index].astype(jnp.float32)
            contrib = jnp.dot(tile.T, hits_float, precision=lax.Precision.HIGHEST)
            active = (slot_index < counts[block_index]).astype(jnp.float32)
            raw_scores = raw_scores.at[targets[block_index, slot_index]].add(active * inverse_block * contrib)
        return raw_scores, None

    initial = jnp.zeros((NT // TBLK, TBLK, NQ), jnp.float32)
    raw_scores, _ = lax.scan(advance, initial, jnp.arange(NBLK, dtype=jnp.int32))
    raw_scores = raw_scores.reshape(NT, NQ)
    target_mean = jnp.sum(raw_scores, axis=1) / NQ
    return raw_scores - target_mean[:, None]
```

```python
import jax
import jax.numpy as jnp
from jax import lax
from jax.experimental import pallas as pl
from jax.experimental.pallas import tpu as pltpu
from jax.sharding import PartitionSpec as P

TBLK = 128
BLOCK = 512
KMAX = 8
NBITS = 2048
WORDS = 64
ROWS = 1024
NBUF = 4
LIB = 8192
STEPS = LIB // ROWS
SLOTS = LIB // BLOCK * KMAX
QL = 128

alpha_weight = 0.7
beta_weight = 0.3
steepness = 16.0

F8 = jnp.float8_e4m3fn
BF = jnp.bfloat16
F32 = jnp.float32
MESH = pl.DeviceIdType.MESH

ORDER = (4, 3, -3, 2, -2, 1, -1, 0)
PLACE = {d: g for g, d in enumerate(ORDER)}
RING0 = ((4, 0), (3, 1), (3, 0), (2, 1), (2, 0), (1, 1), (1, 0))


def kernel(tab, words, cut, lib, tiles, out,
           QQ, LB, TB, S, HT, C, CB, W1, WR, G, CS, CR, M0, M1, YS, YR, F0, FY,
           R0, L0, R1H, L1H, R1, L1, MS, MR, TMP,
           lsem, tsem, g1s, g1r, g2s, g2r, cs, cr, ys, yr, fs, fr,
           r0s, r0r, l0s, l0r, r1s, r1r, l1s, l1r, ms, mr):
    qi = lax.axis_index("query")
    li = lax.axis_index("lib")
    z = li // 4
    p4 = lax.rem(li, 4)
    yl = p4 // 2
    core = lax.rem(p4, 2)

    def lcp(i):
        s = lax.rem(i, NBUF)
        return pltpu.make_async_copy(
            lib.at[pl.ds(pl.multiple_of(i * ROWS, ROWS), ROWS)], LB.at[s], lsem.at[s])

    def tcp(i):
        s = lax.rem(i, NBUF)
        return pltpu.make_async_copy(
            tiles.at[pl.ds(i * (ROWS // BLOCK), ROWS // BLOCK)], TB.at[s], tsem.at[s])

    for i in range(NBUF):
        lcp(i).start()
        tcp(i).start()

    def square(k):
        return (qi, z * 4 + lax.rem(p4 + k, 4))

    def along(k):
        return (qi, lax.rem(z + k + 8, 8) * 4 + p4)

    def other(k):
        return (lax.rem(qi + k, 8), li)

    partners = [square(k) for k in (1, 2, 3)]
    partners += [along(k) for k in range(1, 8)]
    partners += [other(k) for k in range(1, 8)]
    barrier = pltpu.get_barrier_semaphore()
    for dev in partners:
        pl.semaphore_signal(barrier, inc=1, device_id=dev, device_id_type=MESH)
    pl.semaphore_wait(barrier, len(partners))

    def remote(src, dst, ssem, rsem, dev):
        return pltpu.make_async_remote_copy(
            src_ref=src, dst_ref=dst, send_sem=ssem, recv_sem=rsem,
            device_id=dev, device_id_type=MESH)

    sent = []

    def start(copy):
        copy.start()
        sent.append(copy)
        return copy

    one = [start(remote(words, WR.at[k], g1s.at[k], g1r.at[k], square(k + 1)))
           for k in range(3)]

    def cutstep(r, carry):
        for k in range(4):
            row = r * 4 + k
            CB[pl.ds(pl.multiple_of(row * 128, 128), 128), :] = jnp.broadcast_to(
                cut[pl.ds(row, 1), :], (128, 128)).T
        return carry

    for copy in one:
        copy.wait_recv()
    W1[...] = words[...] + WR[0] + WR[1] + WR[2]
    two = [start(remote(W1, G.at[z], g2s.at[k], g2r.at[k], along(k + 1)))
           for k in range(7)]
    G[z] = W1[...]
    C[SLOTS] = jnp.zeros((QL, TBLK), F32)
    QQ[:, QL:2 * QL] = jnp.ones((NBITS, QL), F32).astype(F8)
    lax.fori_loop(0, 16, cutstep, 0)
    for copy in two:
        copy.wait_recv()

    turned = G[...].reshape(64, 128).T
    panel = jnp.concatenate([turned[0:64], turned[64:128]], axis=1)
    shifts = lax.broadcasted_iota(jnp.int32, (WORDS, 32, QL), 1)
    bits = lax.shift_right_logical(
        jnp.broadcast_to(panel[:, None, :], (WORDS, 32, QL)), shifts) & 1
    bits = bits.reshape(NBITS, QL).astype(F32)
    scaled_count = alpha_weight * jnp.sum(bits, axis=0, keepdims=True)
    QQ[:, 0:QL] = bits.astype(F8)

    def step(i, carry):
        s = lax.rem(i, NBUF)
        lcp(i).wait()
        S[...] = jnp.dot(LB[s].astype(F8), QQ[...], preferred_element_type=F32)
        denominator = jnp.maximum(scaled_count + beta_weight * S[:, QL:2 * QL], 1.0)
        similarity = S[:, 0:QL] / denominator
        cutoffs = CB[pl.ds(pl.multiple_of(i * ROWS, ROWS), ROWS), :]
        hits = jax.nn.sigmoid(steepness * (similarity - cutoffs)).astype(BF)
        HT[...] = hits.T
        tcp(i).wait()
        for b in range(ROWS // BLOCK):
            block_hits = HT[:, b * BLOCK:(b + 1) * BLOCK]
            for k in range(0, KMAX, 2):
                slot = (i * (ROWS // BLOCK) + b) * KMAX + k
                pair = jnp.concatenate([TB[s, b, k], TB[s, b, k + 1]], axis=1)
                terms = jnp.dot(block_hits, pair, preferred_element_type=F32)
                C[slot] = terms[:, 0:TBLK] + C[tab[slot]]
                C[slot + 1] = terms[:, TBLK:2 * TBLK] + C[tab[slot + 1]]

        @pl.when(i + NBUF < STEPS)
        def _():
            lcp(i + NBUF).start()
            tcp(i + NBUF).start()

        return carry

    lax.fori_loop(0, STEPS, step, 0)

    def total(g, a, core_of, h):
        zz = lax.rem(z + ORDER[g] + 8, 8)
        yy = lax.rem(yl + a, 2)
        return C[tab[SLOTS + zz * 8 + yy * 4 + core_of * 2 + h]]

    mate = (qi, z * 4 + yl * 2 + (1 - core))
    beside = (qi, z * 4 + (1 - yl) * 2 + core)
    right, left = along(1), along(-1)

    swap = []
    for g in range(8):
        for a in range(2):
            for h in range(2):
                CS[g, a * 2 + h] = total(g, a, 1 - core, h)
        swap.append(start(remote(CS.at[g], CR.at[g], cs.at[g], cr.at[g], mate)))

    across = []
    ring0 = {}
    ring1 = {}

    def send0(d, a):
        n = RING0.index((d, a))
        ring0[d, a] = start(remote(
            M0.at[PLACE[d], a], R0.at[n], r0s.at[n], r0r.at[n], right))

    def send0l(d, a):
        n = RING0.index((d, 1 - a))
        ring0[-d, a] = start(remote(
            M0.at[PLACE[-d if d < 4 else 4], a], L0.at[n], l0s.at[n], l0r.at[n], left))

    def take0(d, a):
        n = RING0.index((d + 1, a))
        ring0[d + 1, a].wait_recv()
        g = PLACE[d]
        M0[g, a] = M0[g, a] + R0[n]

    def take0l(d, a):
        n = RING0.index((d + 1, 1 - a))
        ring0[-(d + 1), a].wait_recv()
        g = PLACE[-d]
        M0[g, a] = M0[g, a] + L0[n]

    def merge(g):
        swap[g].wait_recv()
        YS[g] = total(g, 1, core, 1) + CR[g, 3]
        across.append(start(remote(YS.at[g], YR.at[g], ys.at[g], yr.at[g], beside)))
        M0[g, 0] = total(g, 0, core, 0) + CR[g, 0]
        M0[g, 1] = total(g, 1, core, 0) + CR[g, 2]
        M1[g] = total(g, 0, core, 1) + CR[g, 1]

    def join(g):
        across[g].wait_recv()
        M1[g] = M1[g] + YR[g]

    def far1():
        g = PLACE[4]
        join(g)
        ring1[4] = start(remote(M1.at[g, pl.ds(0, 64)], R1H, r1s.at[3], r1r.at[3], right))
        ring1[-4] = start(remote(M1.at[g, pl.ds(64, 64)], L1H, l1s.at[3], l1r.at[3], left))

    def take1(d):
        g = PLACE[d]
        ring1[d + 1].wait_recv()
        if d == 3:
            M1[g, 0:64] = M1[g, 0:64] + R1H[...]
        else:
            M1[g] = M1[g] + R1[d]

    def take1l(d):
        g = PLACE[-d]
        ring1[-(d + 1)].wait_recv()
        if d == 3:
            M1[g, 64:128] = M1[g, 64:128] + L1H[...]
        else:
            M1[g] = M1[g] + L1[d]

    def send1(d):
        ring1[d] = start(remote(
            M1.at[PLACE[d]], R1.at[d - 1], r1s.at[d - 1], r1r.at[d - 1], right))

    def send1l(d):
        ring1[-d] = start(remote(
            M1.at[PLACE[-d]], L1.at[d - 1], l1s.at[d - 1], l1r.at[d - 1], left))

    merge(0)
    send0(4, 0)
    send0l(4, 1)
    merge(1)
    send0(3, 1)
    merge(2)
    send0l(3, 0)
    take0(3, 0)
    send0(3, 0)
    take0l(3, 1)
    send0l(3, 1)
    merge(3)
    merge(4)
    far1()
    merge(5)
    merge(6)
    merge(7)
    take0(2, 1)
    send0(2, 1)
    take0l(2, 0)
    send0l(2, 0)
    take0(2, 0)
    send0(2, 0)
    take0l(2, 1)
    send0l(2, 1)
    for d in (3,):
        join(PLACE[d])
        take1(d)
        send1(d)
        join(PLACE[-d])
        take1l(d)
        send1l(d)
    take0(1, 1)
    send0(1, 1)
    take0l(1, 0)
    send0l(1, 0)
    take0(1, 0)
    send0(1, 0)
    take0l(1, 1)
    send0l(1, 1)
    for d in (2,):
        join(PLACE[d])
        take1(d)
        send1(d)
        join(PLACE[-d])
        take1l(d)
        send1l(d)
    own = PLACE[0]
    take0(0, 1)
    take0l(0, 1)
    F0[...] = M0[own, 1]
    final = start(remote(F0, FY, fs, fr, beside))
    for d in (1,):
        join(PLACE[d])
        take1(d)
        send1(d)
        join(PLACE[-d])
        take1l(d)
        send1l(d)
    take0(0, 0)
    take0l(0, 0)
    join(own)
    final.wait_recv()
    M0[own, 0] = M0[own, 0] + FY[...]
    MS[0] = jnp.sum(M0[own, 0].reshape(16, 8, 128), axis=0)
    take1(0)
    take1l(0)
    MS[1] = jnp.sum(M1[own].reshape(16, 8, 128), axis=0)

    means = [start(remote(MS, MR.at[k], ms.at[k], mr.at[k], other(k + 1)))
             for k in range(7)]
    for copy in means:
        copy.wait_recv()
    sums = MS[...]
    for k in range(7):
        sums = sums + MR[k]
    mean = jnp.sum(sums, axis=1, keepdims=True) * (1.0 / 1024.0)
    for h in range(2):
        block = M0[own, 0] if h == 0 else M1[own]
        block = (block - mean[h]) * (1.0 / BLOCK)
        TMP[pl.ds(0, 64, stride=2), :] = block[0:64]
        TMP[pl.ds(1, 64, stride=2), :] = block[64:128]
        out[h * TBLK:(h + 1) * TBLK, :] = TMP[...].T
    for copy in sent:
        copy.wait_send()


def local(query_words, lib_bits, cutoff, counts, targets, activity_tiles):
    position = lax.rem(lax.axis_index("lib"), 4)
    packed = jnp.tile(query_words.reshape(2, 128), (4, 1))
    rows = lax.broadcasted_iota(jnp.int32, (8, 128), 0)
    words = jnp.where(rows // 2 == position, packed, 0)

    target = targets.reshape(SLOTS)
    live = (jnp.arange(KMAX, dtype=jnp.int32)[None, :] < counts[:, None]).reshape(SLOTS)
    key = jnp.where(live, target, -1)
    slot = jnp.arange(SLOTS, dtype=jnp.int32)
    wanted = jnp.concatenate([target, jnp.arange(64, dtype=jnp.int32)])
    bound = jnp.concatenate([slot, jnp.full((64,), SLOTS, jnp.int32)])
    named = (wanted[:, None] == key[None, :]) & (slot[None, :] < bound[:, None])
    tab = jnp.max(jnp.where(named, slot[None, :], -1), axis=1)
    tab = jnp.where(tab < 0, SLOTS, tab)

    V = pltpu.VMEM
    dma = pltpu.SemaphoreType.DMA
    block = (QL, TBLK)
    return pl.pallas_call(
        kernel,
        out_shape=jax.ShapeDtypeStruct((2 * TBLK, QL), F32),
        in_specs=[
            pl.BlockSpec(memory_space=pltpu.SMEM),
            pl.BlockSpec(memory_space=V),
            pl.BlockSpec(memory_space=V),
            pl.BlockSpec(memory_space=pl.ANY),
            pl.BlockSpec(memory_space=pl.ANY),
        ],
        out_specs=pl.BlockSpec(memory_space=V),
        scratch_shapes=[
            V((NBITS, 2 * QL), F8),
            V((NBUF, ROWS, NBITS), BF),
            V((NBUF, ROWS // BLOCK, KMAX, BLOCK, TBLK), BF),
            V((ROWS, 2 * QL), F32),
            V((QL, ROWS), BF),
            V((SLOTS + 1,) + block, F32),
            V((LIB, 128), F32),
            V((8, 128), jnp.int32),
            V((3, 8, 128), jnp.int32),
            V((8, 8, 128), jnp.int32),
            V((8, 4) + block, F32),
            V((8, 4) + block, F32),
            V((8, 2) + block, F32),
            V((8,) + block, F32),
            V((8,) + block, F32),
            V((8,) + block, F32),
            V(block, F32),
            V(block, F32),
            V((7,) + block, F32),
            V((7,) + block, F32),
            V((64, TBLK), F32),
            V((64, TBLK), F32),
            V((3,) + block, F32),
            V((3,) + block, F32),
            V((2, 8, 128), F32),
            V((7, 2, 8, 128), F32),
            V(block, F32),
            dma((NBUF,)), dma((NBUF,)),
            dma((3,)), dma((3,)), dma((7,)), dma((7,)),
            dma((8,)), dma((8,)), dma((8,)), dma((8,)),
            dma, dma,
            dma((7,)), dma((7,)), dma((7,)), dma((7,)),
            dma((4,)), dma((4,)), dma((4,)), dma((4,)),
            dma((7,)), dma((7,)),
        ],
        compiler_params=pltpu.CompilerParams(
            collective_id=0, has_side_effects=True, vmem_limit_bytes=60 * 2**20),
        cost_estimate=pl.CostEstimate(
            flops=2 * LIB * NBITS * 2 * QL, bytes_accessed=48 * 2**20,
            transcendentals=LIB * QL),
        name="screen",
    )(tab, words, cutoff.reshape(LIB // 128, 128), lib_bits, activity_tiles)


def solution(mesh):
    in_specs = (
        P(("query", "lib"), None),
        P("lib", None),
        P("lib"),
        P("lib"),
        P("lib", None),
        P("lib", None, None, None),
    )
    out_specs = P("lib", "query")
    return jax.shard_map(local, mesh=mesh, in_specs=in_specs, out_specs=out_specs, check_vma=False)
```

```python
import jax
import jax.numpy as jnp
from jax import lax
from jax.experimental import pallas as pl
from jax.experimental.pallas import tpu as pltpu
from jax.sharding import PartitionSpec as P

TBLK = 128
BLOCK = 512
KMAX = 8
NBITS = 2048
WORDS = 64
ROWS = 1024
NBUF = 4
LIB = 8192
STEPS = LIB // ROWS
SLOTS = LIB // BLOCK * KMAX
QL = 128

alpha_weight = 0.7
beta_weight = 0.3
steepness = 16.0

F8 = jnp.float8_e4m3fn
BF = jnp.bfloat16
F32 = jnp.float32
MESH = pl.DeviceIdType.MESH

ORDER = (4, 3, -3, 2, -2, 1, -1, 0)
PLACE = {d: g for g, d in enumerate(ORDER)}
RING0 = ((4, 0), (3, 1), (3, 0), (2, 1), (2, 0), (1, 1), (1, 0))


def kernel(query_words, cutoff, counts, targets, lib, tiles, out,
           QQ, LB, TB, S, HT, C, W0, CUT, CN, TG, TABV, tab, W, W1, WR, G, CS, CR, M0, M1, YS, YR, F0, FY,
           R0, L0, R1H, L1H, R1, L1, MS, MR, TMP,
           lsem, tsem, isem, tabsem, g1s, g1r, g2s, g2r, cs, cr, ys, yr, fs, fr,
           r0s, r0r, l0s, l0r, r1s, r1r, l1s, l1r, ms, mr):
    qi = lax.axis_index("query")
    li = lax.axis_index("lib")
    z = li // 4
    p4 = lax.rem(li, 4)
    yl = p4 // 2
    core = lax.rem(p4, 2)

    def lcp(i):
        s = lax.rem(i, NBUF)
        return pltpu.make_async_copy(
            lib.at[pl.ds(pl.multiple_of(i * ROWS, ROWS), ROWS)], LB.at[s], lsem.at[s])

    def tcp(i):
        s = lax.rem(i, NBUF)
        return pltpu.make_async_copy(
            tiles.at[pl.ds(i * (ROWS // BLOCK), ROWS // BLOCK)], TB.at[s], tsem.at[s])

    small = [pltpu.make_async_copy(src, dst, isem.at[n]) for n, (src, dst) in enumerate((
        (query_words, W0), (counts, CN), (targets, TG), (cutoff, CUT)))]
    for copy in small:
        copy.start()
    lcp(0).start()
    for i in range(1, NBUF):
        lcp(i).start()
        tcp(i - 1).start()
    tcp(NBUF - 1).start()

    def square(k):
        return (qi, z * 4 + lax.rem(p4 + k, 4))

    def along(k):
        return (qi, lax.rem(z + k + 8, 8) * 4 + p4)

    def other(k):
        return (lax.rem(qi + k, 8), li)

    partners = [square(k) for k in (1, 2, 3)]
    partners += [along(k) for k in range(1, 8)]
    partners += [other(k) for k in range(1, 8)]
    barrier = pltpu.get_barrier_semaphore()
    for dev in partners:
        pl.semaphore_signal(barrier, inc=1, device_id=dev, device_id_type=MESH)
    pl.semaphore_wait(barrier, len(partners))

    def remote(src, dst, ssem, rsem, dev):
        return pltpu.make_async_remote_copy(
            src_ref=src, dst_ref=dst, send_sem=ssem, recv_sem=rsem,
            device_id=dev, device_id_type=MESH)

    sent = []

    def start(copy):
        copy.start()
        sent.append(copy)
        return copy

    small[0].wait()
    rows = lax.broadcasted_iota(jnp.int32, (8, 128), 0)
    W[...] = jnp.zeros((8, 128), jnp.int32)
    for j in range(2):
        row = jnp.concatenate([W0[2 * j:2 * j + 1], W0[2 * j + 1:2 * j + 2]], axis=1)
        W[...] = jnp.where(rows == 2 * p4 + j, jnp.broadcast_to(row, (8, 128)), W[...])
    one = [start(remote(W, WR.at[k], g1s.at[k], g1r.at[k], square(k + 1)))
           for k in range(3)]

    small[1].wait()
    small[2].wait()
    small[3].wait()
    blocks = SLOTS // KMAX
    of_block = (lax.broadcasted_iota(jnp.int32, (SLOTS, blocks), 0) // KMAX
                == lax.broadcasted_iota(jnp.int32, (SLOTS, blocks), 1)).astype(F32)
    spread = lax.dot_general(of_block, TG[...].astype(F32), (((1,), (1,)), ((), ())),
                             preferred_element_type=F32)
    place = lax.broadcasted_iota(jnp.int32, (SLOTS, KMAX), 0) % KMAX
    number = lax.broadcasted_iota(jnp.int32, (SLOTS, KMAX), 1)
    target = jnp.sum(jnp.where(place == number, spread, 0.0), axis=1, keepdims=True)
    live = jnp.sum(of_block * CN[...].astype(F32), axis=1, keepdims=True)
    slot_place = (lax.broadcasted_iota(jnp.int32, (SLOTS, 1), 0) % KMAX).astype(F32)
    key = jnp.where(slot_place < live, target, -1.0)
    keys = jnp.broadcast_to(key, (SLOTS, SLOTS))
    wanted = jnp.broadcast_to(target, (SLOTS, SLOTS)).T
    down = lax.broadcasted_iota(jnp.int32, (SLOTS, SLOTS), 0)
    over = lax.broadcasted_iota(jnp.int32, (SLOTS, SLOTS), 1)
    before = jnp.max(jnp.where((keys == wanted) & (down < over), down, -1),
                     axis=0, keepdims=True)
    final_slot = jnp.max(jnp.where(keys == over.astype(F32), down, -1),
                         axis=0, keepdims=True)
    both = jnp.where(rows == 0, jnp.broadcast_to(before, (8, 128)),
                     jnp.broadcast_to(final_slot, (8, 128)))
    TABV[...] = jnp.where(both < 0, SLOTS, both)
    tabcopy = pltpu.make_async_copy(TABV, tab, tabsem)
    tabcopy.start()

    for copy in one:
        copy.wait_recv()
    W1[...] = W[...] + WR[0] + WR[1] + WR[2]
    two = [start(remote(W1, G.at[z], g2s.at[k], g2r.at[k], along(k + 1)))
           for k in range(7)]
    G[z] = W1[...]
    C[SLOTS] = jnp.zeros((QL, TBLK), F32)
    QQ[:, QL:2 * QL] = jnp.ones((NBITS, QL), F32).astype(F8)
    tabcopy.wait()
    for copy in two:
        copy.wait_recv()

    turned = G[...].reshape(64, 128).T
    panel = jnp.concatenate([turned[0:64], turned[64:128]], axis=1)
    shifts = lax.broadcasted_iota(jnp.int32, (WORDS, 32, QL), 1)
    bits = lax.shift_right_logical(
        jnp.broadcast_to(panel[:, None, :], (WORDS, 32, QL)), shifts) & 1
    bits = bits.reshape(NBITS, QL).astype(F32)
    scaled_count = alpha_weight * jnp.sum(bits, axis=0, keepdims=True)
    QQ[:, 0:QL] = bits.astype(F8)

    def screen(i, S):
        S[...] = jnp.dot(LB[lax.rem(i, NBUF)].astype(F8), QQ[...],
                         preferred_element_type=F32)

    def hit(i, S, HT):
        denominator = jnp.maximum(scaled_count + beta_weight * S[:, QL:2 * QL], 1.0)
        similarity = S[:, 0:QL] / denominator
        cutoffs = jnp.concatenate(
            [jnp.broadcast_to(CUT[pl.ds(i * (ROWS // 128) + k, 1), :], (128, 128)).T
             for k in range(ROWS // 128)], axis=0)
        hits = jax.nn.sigmoid(steepness * (similarity - cutoffs)).astype(BF)
        HT[...] = hits.T

    def gather_terms(i, HT):
        s = lax.rem(i, NBUF)
        for b in range(ROWS // BLOCK):
            block_hits = HT[:, b * BLOCK:(b + 1) * BLOCK]
            for k in range(0, KMAX, 2):
                slot = (i * (ROWS // BLOCK) + b) * KMAX + k
                pair = jnp.concatenate([TB[s, b, k], TB[s, b, k + 1]], axis=1)
                terms = jnp.dot(block_hits, pair, preferred_element_type=F32)
                C[slot] = terms[:, 0:TBLK] + C[tab[0, slot]]
                C[slot + 1] = terms[:, TBLK:2 * TBLK] + C[tab[0, slot + 1]]

    Ss = (S.at[0], S.at[1])
    HTs = (HT.at[0], HT.at[1])
    lcp(0).wait()
    screen(0, Ss[0])
    lcp(NBUF).start()
    hit(0, Ss[0], HTs[0])

    def advance(i, u):
        lcp(i + 1).wait()
        tcp(i).wait()
        screen(i + 1, Ss[1 - u])
        gather_terms(i, HTs[u])
        hit(i + 1, Ss[1 - u], HTs[1 - u])

        @pl.when(i + 1 + NBUF < STEPS)
        def _():
            lcp(i + 1 + NBUF).start()

        @pl.when(i + NBUF < STEPS)
        def _():
            tcp(i + NBUF).start()

    def twice(j, carry):
        advance(2 * j, 0)
        advance(2 * j + 1, 1)
        return carry

    lax.fori_loop(0, STEPS // 2 - 1, twice, 0)
    advance(STEPS - 2, 0)
    tcp(STEPS - 1).wait()
    gather_terms(STEPS - 1, HTs[1])

    def total(g, a, core_of, h):
        zz = lax.rem(z + ORDER[g] + 8, 8)
        yy = lax.rem(yl + a, 2)
        return C[tab[1, zz * 8 + yy * 4 + core_of * 2 + h]]

    mate = (qi, z * 4 + yl * 2 + (1 - core))
    beside = (qi, z * 4 + (1 - yl) * 2 + core)
    right, left = along(1), along(-1)

    swap = []
    for g in range(8):
        for a in range(2):
            for h in range(2):
                CS[g, a * 2 + h] = total(g, a, 1 - core, h)
        swap.append(start(remote(CS.at[g], CR.at[g], cs.at[g], cr.at[g], mate)))

    across = []
    ring0 = {}
    ring1 = {}

    def send0(d, a):
        n = RING0.index((d, a))
        ring0[d, a] = start(remote(
            M0.at[PLACE[d], a], R0.at[n], r0s.at[n], r0r.at[n], right))

    def send0l(d, a):
        n = RING0.index((d, 1 - a))
        ring0[-d, a] = start(remote(
            M0.at[PLACE[-d if d < 4 else 4], a], L0.at[n], l0s.at[n], l0r.at[n], left))

    def take0(d, a):
        n = RING0.index((d + 1, a))
        ring0[d + 1, a].wait_recv()
        g = PLACE[d]
        M0[g, a] = M0[g, a] + R0[n]

    def take0l(d, a):
        n = RING0.index((d + 1, 1 - a))
        ring0[-(d + 1), a].wait_recv()
        g = PLACE[-d]
        M0[g, a] = M0[g, a] + L0[n]

    def merge(g):
        swap[g].wait_recv()
        YS[g] = total(g, 1, core, 1) + CR[g, 3]
        across.append(start(remote(YS.at[g], YR.at[g], ys.at[g], yr.at[g], beside)))
        M0[g, 0] = total(g, 0, core, 0) + CR[g, 0]
        M0[g, 1] = total(g, 1, core, 0) + CR[g, 2]
        M1[g] = total(g, 0, core, 1) + CR[g, 1]

    def join(g):
        across[g].wait_recv()
        M1[g] = M1[g] + YR[g]

    def far1():
        g = PLACE[4]
        join(g)
        ring1[4] = start(remote(M1.at[g, pl.ds(0, 64)], R1H, r1s.at[3], r1r.at[3], right))
        ring1[-4] = start(remote(M1.at[g, pl.ds(64, 64)], L1H, l1s.at[3], l1r.at[3], left))

    def take1(d):
        g = PLACE[d]
        ring1[d + 1].wait_recv()
        if d == 3:
            M1[g, 0:64] = M1[g, 0:64] + R1H[...]
        else:
            M1[g] = M1[g] + R1[d]

    def take1l(d):
        g = PLACE[-d]
        ring1[-(d + 1)].wait_recv()
        if d == 3:
            M1[g, 64:128] = M1[g, 64:128] + L1H[...]
        else:
            M1[g] = M1[g] + L1[d]

    def send1(d):
        ring1[d] = start(remote(
            M1.at[PLACE[d]], R1.at[d - 1], r1s.at[d - 1], r1r.at[d - 1], right))

    def send1l(d):
        ring1[-d] = start(remote(
            M1.at[PLACE[-d]], L1.at[d - 1], l1s.at[d - 1], l1r.at[d - 1], left))

    merge(0)
    send0(4, 0)
    send0l(4, 1)
    merge(1)
    send0(3, 1)
    merge(2)
    send0l(3, 0)
    take0(3, 0)
    send0(3, 0)
    take0l(3, 1)
    send0l(3, 1)
    merge(3)
    merge(4)
    far1()
    merge(5)
    merge(6)
    merge(7)
    take0(2, 1)
    send0(2, 1)
    take0l(2, 0)
    send0l(2, 0)
    take0(2, 0)
    send0(2, 0)
    take0l(2, 1)
    send0l(2, 1)
    for d in (3,):
        join(PLACE[d])
        take1(d)
        send1(d)
        join(PLACE[-d])
        take1l(d)
        send1l(d)
    take0(1, 1)
    send0(1, 1)
    take0l(1, 0)
    send0l(1, 0)
    take0(1, 0)
    send0(1, 0)
    take0l(1, 1)
    send0l(1, 1)
    for d in (2,):
        join(PLACE[d])
        take1(d)
        send1(d)
        join(PLACE[-d])
        take1l(d)
        send1l(d)
    own = PLACE[0]
    take0(0, 1)
    take0l(0, 1)
    F0[...] = M0[own, 1]
    final = start(remote(F0, FY, fs, fr, beside))
    for d in (1,):
        join(PLACE[d])
        take1(d)
        send1(d)
        join(PLACE[-d])
        take1l(d)
        send1l(d)
    take0(0, 0)
    take0l(0, 0)
    join(own)
    final.wait_recv()
    M0[own, 0] = M0[own, 0] + FY[...]
    MS[0] = jnp.sum(M0[own, 0].reshape(16, 8, 128), axis=0)
    take1(0)
    take1l(0)
    MS[1] = jnp.sum(M1[own].reshape(16, 8, 128), axis=0)

    means = [start(remote(MS, MR.at[k], ms.at[k], mr.at[k], other(k + 1)))
             for k in range(7)]
    for copy in means:
        copy.wait_recv()
    sums = MS[...]
    for k in range(7):
        sums = sums + MR[k]
    mean = jnp.sum(sums, axis=1, keepdims=True) * (1.0 / 1024.0)
    for h in range(2):
        block = M0[own, 0] if h == 0 else M1[own]
        block = (block - mean[h]) * (1.0 / BLOCK)
        TMP[pl.ds(0, 64, stride=2), :] = block[0:64]
        TMP[pl.ds(1, 64, stride=2), :] = block[64:128]
        out[h * TBLK:(h + 1) * TBLK, :] = TMP[...].T
    for copy in sent:
        copy.wait_send()


def local(query_words, lib_bits, cutoff, counts, targets, activity_tiles):
    V = pltpu.VMEM
    dma = pltpu.SemaphoreType.DMA
    block = (QL, TBLK)
    return pl.pallas_call(
        kernel,
        out_shape=jax.ShapeDtypeStruct((2 * TBLK, QL), F32),
        in_specs=[pl.BlockSpec(memory_space=pl.ANY)] * 6,
        out_specs=pl.BlockSpec(memory_space=V),
        scratch_shapes=[
            V((NBITS, 2 * QL), F8),
            V((NBUF, ROWS, NBITS), BF),
            V((NBUF, ROWS // BLOCK, KMAX, BLOCK, TBLK), BF),
            V((2, ROWS, 2 * QL), F32),
            V((2, QL, ROWS), BF),
            V((SLOTS + 1,) + block, F32),
            V((4, WORDS), jnp.int32),
            V((LIB // 128, 128), F32),
            V((1, SLOTS // KMAX), jnp.int32),
            V((KMAX, SLOTS // KMAX), jnp.int32),
            V((8, 128), jnp.int32),
            pltpu.SMEM((8, 128), jnp.int32),
            V((8, 128), jnp.int32),
            V((8, 128), jnp.int32),
            V((3, 8, 128), jnp.int32),
            V((8, 8, 128), jnp.int32),
            V((8, 4) + block, F32),
            V((8, 4) + block, F32),
            V((8, 2) + block, F32),
            V((8,) + block, F32),
            V((8,) + block, F32),
            V((8,) + block, F32),
            V(block, F32),
            V(block, F32),
            V((7,) + block, F32),
            V((7,) + block, F32),
            V((64, TBLK), F32),
            V((64, TBLK), F32),
            V((3,) + block, F32),
            V((3,) + block, F32),
            V((2, 8, 128), F32),
            V((7, 2, 8, 128), F32),
            V(block, F32),
            dma((NBUF,)), dma((NBUF,)), dma((4,)), dma,
            dma((3,)), dma((3,)), dma((7,)), dma((7,)),
            dma((8,)), dma((8,)), dma((8,)), dma((8,)),
            dma, dma,
            dma((7,)), dma((7,)), dma((7,)), dma((7,)),
            dma((4,)), dma((4,)), dma((4,)), dma((4,)),
            dma((7,)), dma((7,)),
        ],
        compiler_params=pltpu.CompilerParams(
            collective_id=0, has_side_effects=True, vmem_limit_bytes=60 * 2**20),
        cost_estimate=pl.CostEstimate(
            flops=2 * LIB * NBITS * 2 * QL, bytes_accessed=48 * 2**20,
            transcendentals=LIB * QL),
        name="screen",
    )(query_words, cutoff.reshape(LIB // 128, 128), counts.reshape(1, SLOTS // KMAX),
      targets.T, lib_bits, activity_tiles)


def solution(mesh):
    in_specs = (
        P(("query", "lib"), None),
        P("lib", None),
        P("lib"),
        P("lib"),
        P("lib", None),
        P("lib", None, None, None),
    )
    out_specs = P("lib", "query")
    return jax.shard_map(local, mesh=mesh, in_specs=in_specs, out_specs=out_specs, check_vma=False)
```

```python
import jax
import jax.numpy as jnp
from jax import lax
from jax.experimental import pallas as pl
from jax.experimental.pallas import tpu as pltpu
from jax.sharding import PartitionSpec as P

TBLK = 128
BLOCK = 512
KMAX = 8
NBITS = 2048
WORDS = 64
ROWS = 1024
NBUF = 5
LIB = 8192
STEPS = LIB // ROWS
SLOTS = LIB // BLOCK * KMAX
QL = 128

alpha_weight = 0.7
beta_weight = 0.3
steepness = 16.0

F8 = jnp.float8_e4m3fn
BF = jnp.bfloat16
F32 = jnp.float32
MESH = pl.DeviceIdType.MESH

ORDER = (4, 3, -3, 2, -2, 1, -1, 0)
PLACE = {d: g for g, d in enumerate(ORDER)}
HALF = 64

STEPS_OF_SUM = (
    "S0", "S1", "S2", "S3", "S4", "S5", "S6", "S7", "M0", "L42", "R41", "R40", "L43", "M1",
    "R33", "R32", "M2", "L30", "L31", "M3", "M4", "M5", "M6", "M7", "C1", "J00", "L32", "R31",
    "Rh40", "J01", "Lh41", "L33", "R30", "J10", "L20", "R23", "J11", "Rh31", "L21", "R22",
    "J20", "Lh30", "L22", "R21", "J21", "Lh31", "J30", "Rh30", "L23", "R20", "J31", "C2",
    "L10", "J40", "R13", "L11", "J41", "Rh21", "Lh20", "J50", "R12", "L12", "J51", "R11",
    "Lh21", "Rh20", "J60", "C3", "L13", "J61", "R10", "J70", "J71", "Rh11", "Lh10", "F2",
    "Lh11", "Rh10", "F3", "E00", "E01", "E10", "E11",
)


def kernel(query_words, cutoff, counts, targets, lib, tiles, out,
           QQ, LB, TB, S, HT, C, W0, CUT, CN, TG, TABV, tab, W, W1, WR, G, CS, CR, M0, M1, YS, YR, FY,
           R0, L0, R1, L1, MC, MZ, MX, MY, TMP,
           lsem, tsem, isem, tabsem, g1s, g1r, g2s, g2r, cs, cr, ys, yr, fs, fr,
           r0s, r0r, l0s, l0r, r1s, r1r, l1s, l1r, zs, zr, xs, xr, us, ur):
    qi = lax.axis_index("query")
    li = lax.axis_index("lib")
    z = li // 4
    p4 = lax.rem(li, 4)
    yl = p4 // 2
    core = lax.rem(p4, 2)

    def lcp(i):
        s = lax.rem(i, NBUF)
        return pltpu.make_async_copy(
            lib.at[pl.ds(pl.multiple_of(i * ROWS, ROWS), ROWS)], LB.at[s], lsem.at[s])

    def tcp(i):
        s = lax.rem(i, NBUF)
        return pltpu.make_async_copy(
            tiles.at[pl.ds(i * (ROWS // BLOCK), ROWS // BLOCK)], TB.at[s], tsem.at[s])

    small = [pltpu.make_async_copy(src, dst, isem.at[n]) for n, (src, dst) in enumerate((
        (query_words, W0), (counts, CN), (targets, TG), (cutoff, CUT)))]
    for copy in small:
        copy.start()
    lcp(0).start()
    lcp(1).start()

    def square(k):
        return (qi, z * 4 + lax.rem(p4 + k, 4))

    def along(k):
        return (qi, lax.rem(z + k + 8, 8) * 4 + p4)

    def aside(k):
        return (lax.rem(qi + 2 * k, 8), li)

    high = lax.rem(qi, 2)
    beside = (qi, z * 4 + (1 - yl) * 2 + core)
    over_y = (beside,
              (qi + 1 - 2 * high, li),
              (qi + 1 - 2 * high, z * 4 + (1 - yl) * 2 + core))

    partners = [square(k) for k in (1, 2, 3)]
    partners += [along(k) for k in range(1, 8)]
    partners += [aside(k) for k in range(1, 4)]
    partners += over_y[1:]
    barrier = pltpu.get_barrier_semaphore()
    for dev in partners:
        pl.semaphore_signal(barrier, inc=1, device_id=dev, device_id_type=MESH)

    def remote(src, dst, ssem, rsem, dev):
        return pltpu.make_async_remote_copy(
            src_ref=src, dst_ref=dst, send_sem=ssem, recv_sem=rsem,
            device_id=dev, device_id_type=MESH)

    sent = []

    def start(copy):
        copy.start()
        sent.append(copy)
        return copy

    small[1].wait()
    small[2].wait()
    small[3].wait()
    rows = lax.broadcasted_iota(jnp.int32, (8, 128), 0)
    blocks = SLOTS // KMAX
    of_block = (lax.broadcasted_iota(jnp.int32, (SLOTS, blocks), 0) // KMAX
                == lax.broadcasted_iota(jnp.int32, (SLOTS, blocks), 1)).astype(F32)
    spread = lax.dot_general(of_block, TG[...].astype(F32), (((1,), (1,)), ((), ())),
                             preferred_element_type=F32)
    place = lax.broadcasted_iota(jnp.int32, (SLOTS, KMAX), 0) % KMAX
    number = lax.broadcasted_iota(jnp.int32, (SLOTS, KMAX), 1)
    target = jnp.sum(jnp.where(place == number, spread, 0.0), axis=1, keepdims=True)
    live = jnp.sum(of_block * CN[...].astype(F32), axis=1, keepdims=True)
    slot_place = (lax.broadcasted_iota(jnp.int32, (SLOTS, 1), 0) % KMAX).astype(F32)
    key = jnp.where(slot_place < live, target, -1.0)
    keys = jnp.broadcast_to(key, (SLOTS, SLOTS))
    wanted = jnp.broadcast_to(target, (SLOTS, SLOTS)).T
    down = lax.broadcasted_iota(jnp.int32, (SLOTS, SLOTS), 0)
    over = lax.broadcasted_iota(jnp.int32, (SLOTS, SLOTS), 1)
    before = jnp.max(jnp.where((keys == wanted) & (down < over), down, -1),
                     axis=0, keepdims=True)
    final_slot = jnp.max(jnp.where(keys == over.astype(F32), down, -1),
                         axis=0, keepdims=True)
    both = jnp.where(rows == 0, jnp.broadcast_to(before, (8, 128)),
                     jnp.broadcast_to(final_slot, (8, 128)))
    TABV[...] = jnp.where(both < 0, SLOTS, both)
    tabcopy = pltpu.make_async_copy(TABV, tab, tabsem)
    tabcopy.start()

    tcp(0).start()
    for i in range(2, NBUF):
        lcp(i).start()
        tcp(i - 1).start()
    tcp(NBUF - 1).start()

    small[0].wait()
    W[...] = jnp.zeros((8, 128), jnp.int32)
    for j in range(2):
        row = jnp.concatenate([W0[2 * j:2 * j + 1], W0[2 * j + 1:2 * j + 2]], axis=1)
        W[...] = jnp.where(rows == 2 * p4 + j, jnp.broadcast_to(row, (8, 128)), W[...])
    pl.semaphore_wait(barrier, len(partners))
    one = [start(remote(W, WR.at[k], g1s.at[k], g1r.at[k], square(k + 1)))
           for k in range(3)]
    for copy in one:
        copy.wait_recv()
    W1[...] = W[...] + WR[0] + WR[1] + WR[2]
    two = [start(remote(W1, G.at[z], g2s.at[k], g2r.at[k], along(k + 1)))
           for k in range(7)]
    G[z] = W1[...]
    C[SLOTS] = jnp.zeros((QL, TBLK), F32)
    QQ[:, QL:2 * QL] = jnp.ones((NBITS, QL), F32).astype(F8)
    tabcopy.wait()
    for copy in two:
        copy.wait_recv()

    turned = G[...].reshape(64, 128).T
    panel = jnp.concatenate([turned[0:64], turned[64:128]], axis=1)
    shifts = lax.broadcasted_iota(jnp.int32, (WORDS, 32, QL), 1)
    bits = lax.shift_right_logical(
        jnp.broadcast_to(panel[:, None, :], (WORDS, 32, QL)), shifts) & 1
    bits = bits.reshape(NBITS, QL).astype(F32)
    scaled_count = alpha_weight * jnp.sum(bits, axis=0, keepdims=True)
    QQ[:, 0:QL] = bits.astype(F8)

    def screen(i, S):
        S[...] = jnp.dot(LB[lax.rem(i, NBUF)].astype(F8), QQ[...],
                         preferred_element_type=F32)

    def hit(i, S, HT):
        denominator = jnp.maximum(scaled_count + beta_weight * S[:, QL:2 * QL], 1.0)
        similarity = S[:, 0:QL] / denominator
        cutoffs = jnp.concatenate(
            [jnp.broadcast_to(CUT[pl.ds(i * (ROWS // 128) + k, 1), :], (128, 128)).T
             for k in range(ROWS // 128)], axis=0)
        hits = jax.nn.sigmoid(steepness * (similarity - cutoffs)).astype(BF)
        HT[...] = hits.T

    def gather_terms(i, HT):
        s = lax.rem(i, NBUF)
        for b in range(ROWS // BLOCK):
            block_hits = HT[:, b * BLOCK:(b + 1) * BLOCK]
            for k in range(0, KMAX, 2):
                slot = (i * (ROWS // BLOCK) + b) * KMAX + k
                pair = jnp.concatenate([TB[s, b, k], TB[s, b, k + 1]], axis=1)
                terms = jnp.dot(block_hits, pair, preferred_element_type=F32)
                C[slot] = terms[:, 0:TBLK] + C[tab[0, slot]]
                C[slot + 1] = terms[:, TBLK:2 * TBLK] + C[tab[0, slot + 1]]

    Ss = (S.at[0], S.at[1])
    HTs = (HT.at[0], HT.at[1])
    lcp(0).wait()
    screen(0, Ss[0])
    lcp(NBUF).start()

    def advance(i, u):
        lcp(i + 1).wait()
        tcp(i).wait()
        hit(i, Ss[u], HTs[u])
        screen(i + 1, Ss[1 - u])
        gather_terms(i, HTs[u])

        @pl.when(i + 1 + NBUF < STEPS)
        def _():
            lcp(i + 1 + NBUF).start()

        @pl.when(i + NBUF < STEPS)
        def _():
            tcp(i + NBUF).start()

    def twice(j, carry):
        advance(2 * j, 0)
        advance(2 * j + 1, 1)
        return carry

    lax.fori_loop(0, STEPS // 2 - 1, twice, 0)
    advance(STEPS - 2, 0)
    tcp(STEPS - 1).wait()
    hit(STEPS - 1, Ss[1], HTs[1])
    gather_terms(STEPS - 1, HTs[1])

    def total(g, a, core_of, h):
        zz = lax.rem(z + ORDER[g] + 8, 8)
        yy = lax.rem(yl + a, 2)
        return C[tab[1, zz * 8 + yy * 4 + core_of * 2 + h]]

    mate = (qi, z * 4 + yl * 2 + (1 - core))
    right, left = along(1), along(-1)

    swap, across, ring, last, sums = {}, {}, {}, {}, {}
    own = PLACE[0]
    low = {0: pl.ds(0, HALF), 1: pl.ds(HALF, HALF)}

    def step_S(g):
        for a in range(2):
            for h in range(2):
                CS[g, a * 2 + h] = total(g, a, 1 - core, h)
        swap[g] = start(remote(CS.at[g], CR.at[g], cs.at[g], cr.at[g], mate))

    def by_query(block):
        return jnp.sum(block.reshape(QL // 8, 8, TBLK), axis=0, keepdims=True)

    def step_M(g):
        swap[g].wait_recv()
        far = total(g, 1, core, 1) + CR[g, 3]
        YS[g] = far
        for h in range(2):
            across[g, h] = start(remote(
                YS.at[g, low[h]], YR.at[g, low[h]], ys.at[g, h], yr.at[g, h], beside))
        near0 = total(g, 0, core, 0) + CR[g, 0]
        near1 = total(g, 1, core, 0) + CR[g, 2]
        kept = total(g, 0, core, 1) + CR[g, 1]
        M0[g, 0] = near0
        M0[g, 1] = near1
        M1[g] = kept
        MC[g, 0:4] = jnp.sum(jnp.concatenate(
            [by_query(near0), by_query(kept), by_query(near1), by_query(far)], axis=0), axis=1)

    def step_J(g, h):
        across[g, h].wait_recv()
        M1[g, low[h]] = M1[g, low[h]] + YR[g, low[h]]

    def along_z(way, d, p):
        sign = 1 if way == "R" else -1
        g = PLACE[sign * d if d < 4 else 4]
        buf, ssem, rsem = (R0, r0s, r0r) if way == "R" else (L0, l0s, l0r)
        here = M0.at[g, p // 2, low[p % 2]]
        before = ring.get((way, d + 1, p))
        if before is not None:
            before.wait_recv()
            here[...] = here[...] + buf[d, p]
        if d > 0:
            ring[way, d, p] = start(remote(
                here, buf.at[d - 1, p], ssem.at[d - 1, p], rsem.at[d - 1, p],
                right if way == "R" else left))

    def along_zh(way, d, h):
        sign = 1 if way == "R" else -1
        g = PLACE[sign * d if d < 4 else 4]
        buf, ssem, rsem = (R1, r1s, r1r) if way == "R" else (L1, l1s, l1r)
        here = M1.at[g, low[h]]
        before = ring.get((way + "h", d + 1, h))
        if before is not None:
            before.wait_recv()
            here[...] = here[...] + buf[d, h]
        if d > 0:
            ring[way + "h", d, h] = start(remote(
                here, buf.at[d - 1, h], ssem.at[d - 1, h], rsem.at[d - 1, h],
                right if way == "R" else left))

    def step_F(p):
        along_z("R", 0, p)
        along_z("L", 0, p)
        if p >= 2:
            last[p] = start(remote(
                M0.at[own, 1, low[p - 2]], FY.at[low[p - 2]], fs.at[p - 2], fr.at[p - 2],
                beside))

    def step_E(h, part):
        if h == 0:
            step_F(part)
            last[part + 2].wait_recv()
            M0[own, 0, low[part]] = M0[own, 0, low[part]] + FY[low[part]]
        else:
            along_zh("R", 0, part)
            along_zh("L", 0, part)

    def step_C(n):
        if n == 1:
            for k in range(1, 8):
                g = PLACE[k if k <= 4 else k - 8]
                sums["z", k] = start(remote(
                    MC.at[g], MZ.at[k - 1], zs.at[k - 1], zr.at[k - 1], along(k)))
        elif n == 2:
            rows4 = MC[own]
            for k in range(1, 8):
                sums["z", k].wait_recv()
                rows4 = rows4 + MZ[k - 1]
            MX[3] = rows4
            for k in range(3):
                sums["x", k] = start(remote(
                    MX.at[3], MX.at[k], xs.at[k], xr.at[k], aside(k + 1)))
        else:
            rows4 = MX[3]
            for k in range(3):
                sums["x", k].wait_recv()
                rows4 = rows4 + MX[k]
            MY[3] = rows4
            for k in range(3):
                sums["y", k] = start(remote(
                    MY.at[3], MY.at[k], us.at[k], ur.at[k], over_y[k]))

    MC[...] = jnp.zeros((8, 8, TBLK), F32)
    for name in STEPS_OF_SUM:
        kind, digits = name.rstrip("0123456789"), [int(c) for c in name if c.isdigit()]
        if kind in ("R", "L"):
            along_z(kind, *digits)
        elif kind in ("Rh", "Lh"):
            along_zh(kind[0], *digits)
        else:
            {"S": step_S, "M": step_M, "J": step_J, "F": step_F, "E": step_E,
             "C": step_C}[kind](*digits)

    for k in range(3):
        sums["y", k].wait_recv()
    mean = (MY[3, 0:2] + MY[1, 0:2] + MY[0, 2:4] + MY[2, 2:4]) * (1.0 / 1024.0)
    for h in range(2):
        block = M0[own, 0] if h == 0 else M1[own]
        block = (block - mean[h:h + 1]) * (1.0 / BLOCK)
        TMP[pl.ds(0, 64, stride=2), :] = block[0:64]
        TMP[pl.ds(1, 64, stride=2), :] = block[64:128]
        out[h * TBLK:(h + 1) * TBLK, :] = TMP[...].T
    for copy in sent:
        copy.wait_send()


def local(query_words, lib_bits, cutoff, counts, targets, activity_tiles):
    V = pltpu.VMEM
    dma = pltpu.SemaphoreType.DMA
    block = (QL, TBLK)
    return pl.pallas_call(
        kernel,
        out_shape=pltpu.VMEM((2 * TBLK, QL), F32),
        in_specs=[pl.BlockSpec(memory_space=pl.ANY)] * 6,
        out_specs=pl.BlockSpec(memory_space=V),
        scratch_shapes=[
            V((NBITS, 2 * QL), F8),
            V((NBUF, ROWS, NBITS), BF),
            V((NBUF, ROWS // BLOCK, KMAX, BLOCK, TBLK), BF),
            V((2, ROWS, 2 * QL), F32),
            V((2, QL, ROWS), BF),
            V((SLOTS + 1,) + block, F32),
            V((4, WORDS), jnp.int32),
            V((LIB // 128, 128), F32),
            V((1, SLOTS // KMAX), jnp.int32),
            V((KMAX, SLOTS // KMAX), jnp.int32),
            V((8, 128), jnp.int32),
            pltpu.SMEM((8, 128), jnp.int32),
            V((8, 128), jnp.int32),
            V((8, 128), jnp.int32),
            V((3, 8, 128), jnp.int32),
            V((8, 8, 128), jnp.int32),
            V((8, 4) + block, F32),
            V((8, 4) + block, F32),
            V((8, 2) + block, F32),
            V((8,) + block, F32),
            V((8,) + block, F32),
            V((8,) + block, F32),
            V(block, F32),
            V((4, 4, HALF, TBLK), F32),
            V((4, 4, HALF, TBLK), F32),
            V((4, 2, HALF, TBLK), F32),
            V((4, 2, HALF, TBLK), F32),
            V((8, 8, TBLK), F32),
            V((7, 8, TBLK), F32),
            V((4, 8, TBLK), F32),
            V((4, 8, TBLK), F32),
            V(block, F32),
            dma((NBUF,)), dma((NBUF,)), dma((4,)), dma,
            dma((3,)), dma((3,)), dma((7,)), dma((7,)),
            dma((8,)), dma((8,)), dma((8, 2)), dma((8, 2)),
            dma((2,)), dma((2,)),
            dma((4, 4)), dma((4, 4)), dma((4, 4)), dma((4, 4)),
            dma((4, 2)), dma((4, 2)), dma((4, 2)), dma((4, 2)),
            dma((7,)), dma((7,)), dma((3,)), dma((3,)), dma((3,)), dma((3,)),
        ],
        compiler_params=pltpu.CompilerParams(
            collective_id=0, has_side_effects=True, vmem_limit_bytes=60 * 2**20),
        cost_estimate=pl.CostEstimate(
            flops=2 * LIB * NBITS * 2 * QL, bytes_accessed=48 * 2**20,
            transcendentals=LIB * QL),
        name="screen",
    )(query_words, cutoff.reshape(LIB // 128, 128), counts.reshape(1, SLOTS // KMAX),
      targets.T, lib_bits, activity_tiles)


def solution(mesh):
    in_specs = (
        P(("query", "lib"), None),
        P("lib", None),
        P("lib"),
        P("lib"),
        P("lib", None),
        P("lib", None, None, None),
    )
    out_specs = P("lib", "query")
    return jax.shard_map(local, mesh=mesh, in_specs=in_specs, out_specs=out_specs, check_vma=False)
```

```python
import jax
import jax.numpy as jnp
from jax import lax
from jax.experimental import pallas as pl
from jax.experimental.pallas import tpu as pltpu
from jax.sharding import PartitionSpec as P

TBLK = 128
BLOCK = 512
KMAX = 8
NBITS = 2048
WORDS = 64
ROWS = 1024
NBUF = 5
LIB = 8192
STEPS = LIB // ROWS
SLOTS = LIB // BLOCK * KMAX
QL = 128

alpha_weight = 0.7
beta_weight = 0.3
steepness = 16.0

F8 = jnp.float8_e4m3fn
BF = jnp.bfloat16
F32 = jnp.float32
MESH = pl.DeviceIdType.MESH

ORDER = (4, 3, -3, 2, -2, 1, -1, 0)
PLACE = {d: g for g, d in enumerate(ORDER)}
HALF = 64
FAR = (4, 3, 5, 2, 6, 1, 7)

STEPS_OF_SUM = (
    "S0", "S1", "S2", "S3", "S4", "S5", "S6", "S7", "M0", "L42", "R41", "R40", "L43", "M1",
    "R33", "R32", "M2", "L30", "L31", "M3", "M4", "M5", "M6", "M7", "C1", "J00", "L32", "R31",
    "Rh40", "J01", "Lh41", "L33", "R30", "J10", "L20", "R23", "J11", "Rh31", "L21", "R22",
    "J20", "Lh30", "L22", "R21", "J21", "Lh31", "J30", "Rh30", "L23", "R20", "J31", "C2",
    "L10", "J40", "R13", "L11", "J41", "Rh21", "Lh20", "J50", "R12", "L12", "J51", "R11",
    "Lh21", "Rh20", "J60", "C3", "L13", "J61", "R10", "J70", "J71", "Rh11", "Lh10", "F2",
    "Lh11", "Rh10", "F3", "E10", "E11", "O1", "E00", "E01", "O0",
)


def kernel(query_words, cutoff, counts, targets, lib, tiles, out,
           QQ, LB, TB, S, HT, C, W0, CUT, CN, TG, TABV, tab, W, W1, WR, G, CS, CR, M0, M1, YS, YR, FY,
           R0, L0, R1, L1, MC, MZ, MX, MY, TMP,
           lsem, tsem, isem, tabsem, g1s, g1r, g2s, g2r, cs, cr, ys, yr, fs, fr,
           r0s, r0r, l0s, l0r, r1s, r1r, l1s, l1r, zs, zr, xs, xr, us, ur):
    qi = lax.axis_index("query")
    li = lax.axis_index("lib")
    z = li // 4
    p4 = lax.rem(li, 4)
    yl = p4 // 2
    core = lax.rem(p4, 2)

    def square(k):
        return (qi, z * 4 + lax.rem(p4 + k, 4))

    def along(k):
        return (qi, lax.rem(z + k + 8, 8) * 4 + p4)

    def aside(k):
        return (lax.rem(qi + 2 * k, 8), li)

    high = lax.rem(qi, 2)
    beside = (qi, z * 4 + (1 - yl) * 2 + core)
    over_y = (beside,
              (qi + 1 - 2 * high, li),
              (qi + 1 - 2 * high, z * 4 + (1 - yl) * 2 + core))

    group = [(qi, lax.rem(z + k, 8) * 4 + lax.rem(p4 + m, 4))
             for k in FAR + (0,) for m in (2, 3, 1, 0) if k or m]
    partners = list(group)
    partners += [aside(k) for k in range(1, 4)]
    partners += over_y[1:]
    barrier = pltpu.get_barrier_semaphore()
    for dev in partners:
        pl.semaphore_signal(barrier, inc=1, device_id=dev, device_id_type=MESH)

    def lcp(i):
        s = lax.rem(i, NBUF)
        return pltpu.make_async_copy(
            lib.at[pl.ds(pl.multiple_of(i * ROWS, ROWS), ROWS)], LB.at[s], lsem.at[s])

    def tcp(i):
        s = lax.rem(i, NBUF)
        return pltpu.make_async_copy(
            tiles.at[pl.ds(i * (ROWS // BLOCK), ROWS // BLOCK)], TB.at[s], tsem.at[s])

    small = [pltpu.make_async_copy(src, dst, isem.at[n]) for n, (src, dst) in enumerate((
        (query_words, W0), (counts, CN), (targets, TG), (cutoff, CUT)))]
    for copy in small:
        copy.start()
    lcp(0).start()
    lcp(1).start()

    def remote(src, dst, ssem, rsem, dev):
        return pltpu.make_async_remote_copy(
            src_ref=src, dst_ref=dst, send_sem=ssem, recv_sem=rsem,
            device_id=dev, device_id_type=MESH)

    sent = []

    def start(copy):
        copy.start()
        sent.append(copy)
        return copy

    small[1].wait()
    small[2].wait()
    small[3].wait()
    rows = lax.broadcasted_iota(jnp.int32, (8, 128), 0)
    blocks = SLOTS // KMAX
    of_block = (lax.broadcasted_iota(jnp.int32, (SLOTS, blocks), 0) // KMAX
                == lax.broadcasted_iota(jnp.int32, (SLOTS, blocks), 1)).astype(F32)
    spread = lax.dot_general(of_block, TG[...].astype(F32), (((1,), (1,)), ((), ())),
                             preferred_element_type=F32)
    place = lax.broadcasted_iota(jnp.int32, (SLOTS, KMAX), 0) % KMAX
    number = lax.broadcasted_iota(jnp.int32, (SLOTS, KMAX), 1)
    target = jnp.sum(jnp.where(place == number, spread, 0.0), axis=1, keepdims=True)
    live = jnp.sum(of_block * CN[...].astype(F32), axis=1, keepdims=True)
    slot_place = (lax.broadcasted_iota(jnp.int32, (SLOTS, 1), 0) % KMAX).astype(F32)
    key = jnp.where(slot_place < live, target, -1.0)
    keys = jnp.broadcast_to(key, (SLOTS, SLOTS))
    wanted = jnp.broadcast_to(target, (SLOTS, SLOTS)).T
    down = lax.broadcasted_iota(jnp.int32, (SLOTS, SLOTS), 0)
    over = lax.broadcasted_iota(jnp.int32, (SLOTS, SLOTS), 1)
    before = jnp.max(jnp.where((keys == wanted) & (down < over), down, -1),
                     axis=0, keepdims=True)
    final_slot = jnp.max(jnp.where(keys == over.astype(F32), down, -1),
                         axis=0, keepdims=True)
    both = jnp.where(rows == 0, jnp.broadcast_to(before, (8, 128)),
                     jnp.broadcast_to(final_slot, (8, 128)))
    TABV[...] = jnp.where(both < 0, SLOTS, both)
    tabcopy = pltpu.make_async_copy(TABV, tab, tabsem)
    tabcopy.start()

    tcp(0).start()
    for i in range(2, NBUF):
        lcp(i).start()
        tcp(i - 1).start()
    tcp(NBUF - 1).start()

    small[0].wait()
    W[...] = jnp.zeros((8, 128), jnp.int32)
    for j in range(2):
        row = jnp.concatenate([W0[2 * j:2 * j + 1], W0[2 * j + 1:2 * j + 2]], axis=1)
        W[...] = jnp.where(rows == 2 * p4 + j, jnp.broadcast_to(row, (8, 128)), W[...])
    pl.semaphore_wait(barrier, len(partners))
    two = [start(remote(W, G.at[p4, z], g2s.at[k], g2r.at[k], dev))
           for k, dev in enumerate(group)]
    G[p4, z] = W[...]
    C[SLOTS] = jnp.zeros((QL, TBLK), F32)
    QQ[:, QL:2 * QL] = jnp.ones((NBITS, QL), F32).astype(F8)
    tabcopy.wait()
    for copy in two:
        copy.wait_recv()

    turned = (G[0] + G[1] + G[2] + G[3]).reshape(64, 128).T
    panel = jnp.concatenate([turned[0:64], turned[64:128]], axis=1)
    shifts = lax.broadcasted_iota(jnp.int32, (WORDS, 32, QL), 1)
    bits = lax.shift_right_logical(
        jnp.broadcast_to(panel[:, None, :], (WORDS, 32, QL)), shifts) & 1
    bits = bits.reshape(NBITS, QL).astype(F32)
    scaled_count = alpha_weight * jnp.sum(bits, axis=0, keepdims=True)
    QQ[:, 0:QL] = bits.astype(F8)

    def screen(i, S):
        S[...] = jnp.dot(LB[lax.rem(i, NBUF)].astype(F8), QQ[...],
                         preferred_element_type=F32)

    def hit(i, S, HT):
        denominator = jnp.maximum(scaled_count + beta_weight * S[:, QL:2 * QL], 1.0)
        similarity = S[:, 0:QL] / denominator
        cutoffs = jnp.concatenate(
            [jnp.broadcast_to(CUT[pl.ds(i * (ROWS // 128) + k, 1), :], (128, 128)).T
             for k in range(ROWS // 128)], axis=0)
        hits = jax.nn.sigmoid(steepness * (similarity - cutoffs)).astype(BF)
        HT[...] = hits.T

    def gather_terms(i, HT):
        s = lax.rem(i, NBUF)
        for b in range(ROWS // BLOCK):
            block_hits = HT[:, b * BLOCK:(b + 1) * BLOCK]
            for k in range(0, KMAX, 2):
                slot = (i * (ROWS // BLOCK) + b) * KMAX + k
                pair = jnp.concatenate([TB[s, b, k], TB[s, b, k + 1]], axis=1)
                terms = jnp.dot(block_hits, pair, preferred_element_type=F32)
                C[slot] = terms[:, 0:TBLK] + C[tab[0, slot]]
                C[slot + 1] = terms[:, TBLK:2 * TBLK] + C[tab[0, slot + 1]]

    Ss = (S.at[0], S.at[1])
    HTs = (HT.at[0], HT.at[1])
    lcp(0).wait()
    screen(0, Ss[0])
    lcp(NBUF).start()

    def advance(i, u):
        lcp(i + 1).wait()
        tcp(i).wait()
        hit(i, Ss[u], HTs[u])
        screen(i + 1, Ss[1 - u])
        gather_terms(i, HTs[u])

        @pl.when(i + 1 + NBUF < STEPS)
        def _():
            lcp(i + 1 + NBUF).start()

        @pl.when(i + NBUF < STEPS)
        def _():
            tcp(i + NBUF).start()

    def twice(j, carry):
        advance(2 * j, 0)
        advance(2 * j + 1, 1)
        return carry

    lax.fori_loop(0, STEPS // 2 - 1, twice, 0)
    advance(STEPS - 2, 0)
    tcp(STEPS - 1).wait()
    hit(STEPS - 1, Ss[1], HTs[1])
    gather_terms(STEPS - 1, HTs[1])

    def total(g, a, core_of, h):
        zz = lax.rem(z + ORDER[g] + 8, 8)
        yy = lax.rem(yl + a, 2)
        return C[tab[1, zz * 8 + yy * 4 + core_of * 2 + h]]

    mate = (qi, z * 4 + yl * 2 + (1 - core))
    right, left = along(1), along(-1)

    swap, across, ring, last, sums = {}, {}, {}, {}, {}
    own = PLACE[0]
    low = {0: pl.ds(0, HALF), 1: pl.ds(HALF, HALF)}

    def step_S(g):
        for a in range(2):
            for h in range(2):
                CS[g, a * 2 + h] = total(g, a, 1 - core, h)
        swap[g] = start(remote(CS.at[g], CR.at[g], cs.at[g], cr.at[g], mate))

    def by_query(block):
        return jnp.sum(block.reshape(QL // 8, 8, TBLK), axis=0, keepdims=True)

    def step_M(g):
        swap[g].wait_recv()
        far = total(g, 1, core, 1) + CR[g, 3]
        YS[g] = far
        for h in range(2):
            across[g, h] = start(remote(
                YS.at[g, low[h]], YR.at[g, low[h]], ys.at[g, h], yr.at[g, h], beside))
        near0 = total(g, 0, core, 0) + CR[g, 0]
        near1 = total(g, 1, core, 0) + CR[g, 2]
        kept = total(g, 0, core, 1) + CR[g, 1]
        M0[g, 0] = near0
        M0[g, 1] = near1
        M1[g] = kept
        MC[g, 0:4] = jnp.sum(jnp.concatenate(
            [by_query(near0), by_query(kept), by_query(near1), by_query(far)], axis=0), axis=1)

    def step_J(g, h):
        across[g, h].wait_recv()
        M1[g, low[h]] = M1[g, low[h]] + YR[g, low[h]]

    def along_z(way, d, p):
        sign = 1 if way == "R" else -1
        g = PLACE[sign * d if d < 4 else 4]
        buf, ssem, rsem = (R0, r0s, r0r) if way == "R" else (L0, l0s, l0r)
        here = M0.at[g, p // 2, low[p % 2]]
        before = ring.get((way, d + 1, p))
        if before is not None:
            before.wait_recv()
            here[...] = here[...] + buf[d, p]
        if d > 0:
            ring[way, d, p] = start(remote(
                here, buf.at[d - 1, p], ssem.at[d - 1, p], rsem.at[d - 1, p],
                right if way == "R" else left))

    def along_zh(way, d, h):
        sign = 1 if way == "R" else -1
        g = PLACE[sign * d if d < 4 else 4]
        buf, ssem, rsem = (R1, r1s, r1r) if way == "R" else (L1, l1s, l1r)
        here = M1.at[g, low[h]]
        before = ring.get((way + "h", d + 1, h))
        if before is not None:
            before.wait_recv()
            here[...] = here[...] + buf[d, h]
        if d > 0:
            ring[way + "h", d, h] = start(remote(
                here, buf.at[d - 1, h], ssem.at[d - 1, h], rsem.at[d - 1, h],
                right if way == "R" else left))

    def step_F(p):
        along_z("R", 0, p)
        along_z("L", 0, p)
        if p >= 2:
            last[p] = start(remote(
                M0.at[own, 1, low[p - 2]], FY.at[low[p - 2]], fs.at[p - 2], fr.at[p - 2],
                beside))

    def step_E(h, part):
        if h == 0:
            step_F(part)
            last[part + 2].wait_recv()
            M0[own, 0, low[part]] = M0[own, 0, low[part]] + FY[low[part]]
        else:
            along_zh("R", 0, part)
            along_zh("L", 0, part)

    def step_C(n):
        if n == 1:
            for k in range(1, 8):
                g = PLACE[k if k <= 4 else k - 8]
                sums["z", k] = start(remote(
                    MC.at[g], MZ.at[k - 1], zs.at[k - 1], zr.at[k - 1], along(k)))
        elif n == 2:
            rows4 = MC[own]
            for k in range(1, 8):
                sums["z", k].wait_recv()
                rows4 = rows4 + MZ[k - 1]
            MX[3] = rows4
            for k in range(3):
                sums["x", k] = start(remote(
                    MX.at[3], MX.at[k], xs.at[k], xr.at[k], aside(k + 1)))
        else:
            rows4 = MX[3]
            for k in range(3):
                sums["x", k].wait_recv()
                rows4 = rows4 + MX[k]
            MY[3] = rows4
            for k in range(3):
                sums["y", k] = start(remote(
                    MY.at[3], MY.at[k], us.at[k], ur.at[k], over_y[k]))

    def step_O(h):
        if h == 1:
            for k in range(3):
                sums["y", k].wait_recv()
        mean = (MY[3, h:h + 1] + MY[1, h:h + 1] + MY[0, 2 + h:3 + h]
                + MY[2, 2 + h:3 + h]) * (1.0 / 1024.0)
        block = ((M0[own, 0] if h == 0 else M1[own]) - mean) * (1.0 / BLOCK)
        TMP[pl.ds(0, 64, stride=2), :] = block[0:64]
        TMP[pl.ds(1, 64, stride=2), :] = block[64:128]
        out[h * TBLK:(h + 1) * TBLK, :] = TMP[...].T

    MC[...] = jnp.zeros((8, 8, TBLK), F32)
    for name in STEPS_OF_SUM:
        kind, digits = name.rstrip("0123456789"), [int(c) for c in name if c.isdigit()]
        if kind in ("R", "L"):
            along_z(kind, *digits)
        elif kind in ("Rh", "Lh"):
            along_zh(kind[0], *digits)
        else:
            {"S": step_S, "M": step_M, "J": step_J, "F": step_F, "E": step_E,
             "C": step_C, "O": step_O}[kind](*digits)

    for copy in sent:
        copy.wait_send()


def local(query_words, lib_bits, cutoff, counts, targets, activity_tiles):
    V = pltpu.VMEM
    dma = pltpu.SemaphoreType.DMA
    block = (QL, TBLK)
    return pl.pallas_call(
        kernel,
        out_shape=pltpu.VMEM((2 * TBLK, QL), F32),
        in_specs=[pl.BlockSpec(memory_space=pl.ANY)] * 6,
        out_specs=pl.BlockSpec(memory_space=V),
        scratch_shapes=[
            V((NBITS, 2 * QL), F8),
            V((NBUF, ROWS, NBITS), BF),
            V((NBUF, ROWS // BLOCK, KMAX, BLOCK, TBLK), BF),
            V((2, ROWS, 2 * QL), F32),
            V((2, QL, ROWS), BF),
            V((SLOTS + 1,) + block, F32),
            V((4, WORDS), jnp.int32),
            V((LIB // 128, 128), F32),
            V((1, SLOTS // KMAX), jnp.int32),
            V((KMAX, SLOTS // KMAX), jnp.int32),
            V((8, 128), jnp.int32),
            pltpu.SMEM((8, 128), jnp.int32),
            V((8, 128), jnp.int32),
            V((8, 128), jnp.int32),
            V((3, 8, 128), jnp.int32),
            V((4, 8, 8, 128), jnp.int32),
            V((8, 4) + block, F32),
            V((8, 4) + block, F32),
            V((8, 2) + block, F32),
            V((8,) + block, F32),
            V((8,) + block, F32),
            V((8,) + block, F32),
            V(block, F32),
            V((4, 4, HALF, TBLK), F32),
            V((4, 4, HALF, TBLK), F32),
            V((4, 2, HALF, TBLK), F32),
            V((4, 2, HALF, TBLK), F32),
            V((8, 8, TBLK), F32),
            V((7, 8, TBLK), F32),
            V((4, 8, TBLK), F32),
            V((4, 8, TBLK), F32),
            V(block, F32),
            dma((NBUF,)), dma((NBUF,)), dma((4,)), dma,
            dma((3,)), dma((3,)), dma((31,)), dma((31,)),
            dma((8,)), dma((8,)), dma((8, 2)), dma((8, 2)),
            dma((2,)), dma((2,)),
            dma((4, 4)), dma((4, 4)), dma((4, 4)), dma((4, 4)),
            dma((4, 2)), dma((4, 2)), dma((4, 2)), dma((4, 2)),
            dma((7,)), dma((7,)), dma((3,)), dma((3,)), dma((3,)), dma((3,)),
        ],
        compiler_params=pltpu.CompilerParams(
            collective_id=0, has_side_effects=True, vmem_limit_bytes=60 * 2**20),
        cost_estimate=pl.CostEstimate(
            flops=2 * LIB * NBITS * 2 * QL, bytes_accessed=48 * 2**20,
            transcendentals=LIB * QL),
        name="screen",
    )(query_words, cutoff.reshape(LIB // 128, 128), counts.reshape(1, SLOTS // KMAX),
      targets.T, lib_bits, activity_tiles)


def solution(mesh):
    in_specs = (
        P(("query", "lib"), None),
        P("lib", None),
        P("lib"),
        P("lib"),
        P("lib", None),
        P("lib", None, None, None),
    )
    out_specs = P("lib", "query")
    return jax.shard_map(local, mesh=mesh, in_specs=in_specs, out_specs=out_specs, check_vma=False)
```

```python
import jax
import jax.numpy as jnp
from jax import lax
from jax.experimental import pallas as pl
from jax.experimental.pallas import tpu as pltpu
from jax.sharding import PartitionSpec as P

TBLK = 128
BLOCK = 512
KMAX = 8
NBITS = 2048
WORDS = 64
ROWS = 1024
NBUF = 5
LIB = 8192
STEPS = LIB // ROWS
SLOTS = LIB // BLOCK * KMAX
QL = 128

alpha_weight = 0.7
beta_weight = 0.3
steepness = 16.0

F8 = jnp.float8_e4m3fn
BF = jnp.bfloat16
F32 = jnp.float32
MESH = pl.DeviceIdType.MESH

ORDER = (4, 3, -3, 2, -2, 1, -1, 0)
PLACE = {d: g for g, d in enumerate(ORDER)}
HALF = 64
FAR = (4, 3, 5, 2, 6, 1, 7)

STEPS_OF_SUM = (
    "S0", "S1", "S2", "S3", "S4", "S5", "S6", "S7", "M0", "L42", "R41", "R40", "L43", "M1",
    "R33", "R32", "M2", "L30", "L31", "M3", "M4", "M5", "M6", "M7", "C1", "J00", "L32", "R31",
    "Rh40", "J01", "Lh41", "L33", "R30", "J10", "L20", "R23", "J11", "Rh31", "L21", "R22",
    "J20", "Lh30", "L22", "R21", "J21", "Lh31", "J30", "Rh30", "L23", "R20", "J31", "C2",
    "L10", "J40", "R13", "L11", "J41", "Rh21", "Lh20", "J50", "R12", "L12", "J51", "R11",
    "Lh21", "Rh20", "J60", "C3", "L13", "J61", "R10", "J70", "J71", "Rh11", "Lh10", "F2",
    "Lh11", "Rh10", "F3", "E10", "E11", "O1", "E00", "E01", "O0",
)


def kernel(query_words, cutoff, counts, targets, lib, tiles, out,
           QQ, LB, TB, S, HT, C, W0, CUT, CN, TG, TABV, tab, W, W1, WR, G, CS, CR, M0, M1, YS, YR, FY,
           R0, L0, R1, L1, MC, MZ, MX, MY, TMP,
           lsem, tsem, isem, tabsem, g1s, g1r, g2s, g2r, cs, cr, ys, yr, fs, fr,
           r0s, r0r, l0s, l0r, r1s, r1r, l1s, l1r, zs, zr, xs, xr, us, ur):
    qi = lax.axis_index("query")
    li = lax.axis_index("lib")
    z = li // 4
    p4 = lax.rem(li, 4)
    yl = p4 // 2
    core = lax.rem(p4, 2)

    def square(k):
        return (qi, z * 4 + lax.rem(p4 + k, 4))

    def along(k):
        return (qi, lax.rem(z + k + 8, 8) * 4 + p4)

    def aside(k):
        return (lax.rem(qi + 2 * k, 8), li)

    high = lax.rem(qi, 2)
    beside = (qi, z * 4 + (1 - yl) * 2 + core)
    over_y = (beside,
              (qi + 1 - 2 * high, li),
              (qi + 1 - 2 * high, z * 4 + (1 - yl) * 2 + core))

    group = [(qi, lax.rem(z + k, 8) * 4 + lax.rem(p4 + m, 4))
             for k in FAR + (0,) for m in (2, 3, 1, 0) if k or m]
    partners = list(group)
    partners += [aside(k) for k in range(1, 4)]
    partners += over_y[1:]
    barrier = pltpu.get_barrier_semaphore()
    for dev in partners:
        pl.semaphore_signal(barrier, inc=1, device_id=dev, device_id_type=MESH)

    def lcp(i):
        s = lax.rem(i, NBUF)
        return pltpu.make_async_copy(
            lib.at[pl.ds(pl.multiple_of(i * ROWS, ROWS), ROWS)], LB.at[s], lsem.at[s])

    def tcp(i):
        s = lax.rem(i, NBUF)
        return pltpu.make_async_copy(
            tiles.at[pl.ds(i * (ROWS // BLOCK), ROWS // BLOCK)], TB.at[s], tsem.at[s])

    small = [pltpu.make_async_copy(src, dst, isem.at[n]) for n, (src, dst) in enumerate((
        (query_words, W0), (counts, CN), (targets, TG), (cutoff, CUT)))]
    for copy in small:
        copy.start()
    lcp(0).start()
    lcp(1).start()

    def remote(src, dst, ssem, rsem, dev):
        return pltpu.make_async_remote_copy(
            src_ref=src, dst_ref=dst, send_sem=ssem, recv_sem=rsem,
            device_id=dev, device_id_type=MESH)

    sent = []

    def start(copy):
        copy.start()
        sent.append(copy)
        return copy

    small[1].wait()
    small[2].wait()
    small[3].wait()
    rows = lax.broadcasted_iota(jnp.int32, (8, 128), 0)
    blocks = SLOTS // KMAX
    of_block = (lax.broadcasted_iota(jnp.int32, (SLOTS, blocks), 0) // KMAX
                == lax.broadcasted_iota(jnp.int32, (SLOTS, blocks), 1)).astype(F32)
    spread = lax.dot_general(of_block, TG[...].astype(F32), (((1,), (1,)), ((), ())),
                             preferred_element_type=F32)
    place = lax.broadcasted_iota(jnp.int32, (SLOTS, KMAX), 0) % KMAX
    number = lax.broadcasted_iota(jnp.int32, (SLOTS, KMAX), 1)
    target = jnp.sum(jnp.where(place == number, spread, 0.0), axis=1, keepdims=True)
    live = jnp.sum(of_block * CN[...].astype(F32), axis=1, keepdims=True)
    slot_place = (lax.broadcasted_iota(jnp.int32, (SLOTS, 1), 0) % KMAX).astype(F32)
    key = jnp.where(slot_place < live, target, -1.0)
    keys = jnp.broadcast_to(key, (SLOTS, SLOTS))
    wanted = jnp.broadcast_to(target, (SLOTS, SLOTS)).T
    down = lax.broadcasted_iota(jnp.int32, (SLOTS, SLOTS), 0)
    over = lax.broadcasted_iota(jnp.int32, (SLOTS, SLOTS), 1)
    before = jnp.max(jnp.where((keys == wanted) & (down < over), down, -1),
                     axis=0, keepdims=True)
    final_slot = jnp.max(jnp.where(keys == over.astype(F32), down, -1),
                         axis=0, keepdims=True)
    both = jnp.where(rows == 0, jnp.broadcast_to(before, (8, 128)),
                     jnp.broadcast_to(final_slot, (8, 128)))
    TABV[...] = jnp.where(both < 0, SLOTS, both)
    tabcopy = pltpu.make_async_copy(TABV, tab, tabsem)
    tabcopy.start()

    tcp(0).start()
    for i in range(2, NBUF):
        lcp(i).start()
        tcp(i - 1).start()
    tcp(NBUF - 1).start()

    small[0].wait()
    W[...] = jnp.zeros((8, 128), jnp.int32)
    for j in range(2):
        row = jnp.concatenate([W0[2 * j:2 * j + 1], W0[2 * j + 1:2 * j + 2]], axis=1)
        W[...] = jnp.where(rows == 2 * p4 + j, jnp.broadcast_to(row, (8, 128)), W[...])
    pl.semaphore_wait(barrier, len(partners))
    two = [start(remote(W, G.at[p4, z], g2s.at[k], g2r.at[k], dev))
           for k, dev in enumerate(group)]
    G[p4, z] = W[...]
    C[SLOTS] = jnp.zeros((QL, TBLK), F32)
    QQ[:, QL:2 * QL] = jnp.ones((NBITS, QL), F32).astype(F8)
    tabcopy.wait()
    for copy in two:
        copy.wait_recv()

    turned = (G[0] + G[1] + G[2] + G[3]).reshape(64, 128).T
    panel = jnp.concatenate([turned[0:64], turned[64:128]], axis=1)
    shifts = lax.broadcasted_iota(jnp.int32, (WORDS, 32, QL), 1)
    bits = lax.shift_right_logical(
        jnp.broadcast_to(panel[:, None, :], (WORDS, 32, QL)), shifts) & 1
    bits = bits.reshape(NBITS, QL).astype(F32)
    scaled_count = alpha_weight * jnp.sum(bits, axis=0, keepdims=True)
    QQ[:, 0:QL] = bits.astype(F8)

    def screen(i, S):
        S[...] = jnp.dot(LB[lax.rem(i, NBUF)].astype(F8), QQ[...],
                         preferred_element_type=F32)

    def hit(i, S, HT):
        denominator = jnp.maximum(scaled_count + beta_weight * S[:, QL:2 * QL], 1.0)
        similarity = S[:, 0:QL] / denominator
        cutoffs = jnp.concatenate(
            [jnp.broadcast_to(CUT[pl.ds(i * (ROWS // 128) + k, 1), :], (128, 128)).T
             for k in range(ROWS // 128)], axis=0)
        hits = jax.nn.sigmoid(steepness * (similarity - cutoffs)).astype(BF)
        HT[...] = hits.T

    def gather_terms(i, HT):
        s = lax.rem(i, NBUF)
        for b in range(ROWS // BLOCK):
            block_hits = HT[:, b * BLOCK:(b + 1) * BLOCK]
            for k in range(0, KMAX, 2):
                slot = (i * (ROWS // BLOCK) + b) * KMAX + k
                pair = jnp.concatenate([TB[s, b, k], TB[s, b, k + 1]], axis=1)
                terms = jnp.dot(block_hits, pair, preferred_element_type=F32)
                C[slot] = terms[:, 0:TBLK] + C[tab[0, slot]]
                C[slot + 1] = terms[:, TBLK:2 * TBLK] + C[tab[0, slot + 1]]

    Ss = (S.at[0], S.at[1])
    HTs = (HT.at[0], HT.at[1])
    lcp(0).wait()
    screen(0, Ss[0])
    lcp(NBUF).start()

    def advance(i, u, more=True):
        lcp(i + 1).wait()
        tcp(i).wait()
        hit(i, Ss[u], HTs[u])
        screen(i + 1, Ss[1 - u])
        gather_terms(i, HTs[u])

        if not more:
            return

        @pl.when(i + 1 + NBUF < STEPS)
        def _():
            lcp(i + 1 + NBUF).start()

        @pl.when(i + NBUF < STEPS)
        def _():
            tcp(i + NBUF).start()

    def twice(j, carry):
        advance(2 * j, 0)
        advance(2 * j + 1, 1)
        return carry

    lax.fori_loop(0, STEPS // 2 - 1, twice, 0)
    advance(STEPS - 2, 0, more=False)
    tcp(STEPS - 1).wait()
    hit(STEPS - 1, Ss[1], HTs[1])
    gather_terms(STEPS - 1, HTs[1])

    def total(g, a, core_of, h):
        zz = lax.rem(z + ORDER[g] + 8, 8)
        yy = lax.rem(yl + a, 2)
        return C[tab[1, zz * 8 + yy * 4 + core_of * 2 + h]]

    mate = (qi, z * 4 + yl * 2 + (1 - core))
    right, left = along(1), along(-1)

    swap, across, ring, last, sums = {}, {}, {}, {}, {}
    own = PLACE[0]
    low = {0: pl.ds(0, HALF), 1: pl.ds(HALF, HALF)}

    def step_S(g):
        for a in range(2):
            for h in range(2):
                CS[g, a * 2 + h] = total(g, a, 1 - core, h)
        swap[g] = start(remote(CS.at[g], CR.at[g], cs.at[g], cr.at[g], mate))

    def by_query(block):
        return jnp.sum(block.reshape(QL // 8, 8, TBLK), axis=0, keepdims=True)

    def step_M(g):
        swap[g].wait_recv()
        far = total(g, 1, core, 1) + CR[g, 3]
        YS[g] = far
        for h in range(2):
            across[g, h] = start(remote(
                YS.at[g, low[h]], YR.at[g, low[h]], ys.at[g, h], yr.at[g, h], beside))
        near0 = total(g, 0, core, 0) + CR[g, 0]
        near1 = total(g, 1, core, 0) + CR[g, 2]
        kept = total(g, 0, core, 1) + CR[g, 1]
        M0[g, 0] = near0
        M0[g, 1] = near1
        M1[g] = kept
        MC[g, 0:4] = jnp.sum(jnp.concatenate(
            [by_query(near0), by_query(kept), by_query(near1), by_query(far)], axis=0), axis=1)

    def step_J(g, h):
        across[g, h].wait_recv()
        M1[g, low[h]] = M1[g, low[h]] + YR[g, low[h]]

    def along_z(way, d, p):
        sign = 1 if way == "R" else -1
        g = PLACE[sign * d if d < 4 else 4]
        buf, ssem, rsem = (R0, r0s, r0r) if way == "R" else (L0, l0s, l0r)
        here = M0.at[g, p // 2, low[p % 2]]
        before = ring.get((way, d + 1, p))
        if before is not None:
            before.wait_recv()
            here[...] = here[...] + buf[d, p]
        if d > 0:
            ring[way, d, p] = start(remote(
                here, buf.at[d - 1, p], ssem.at[d - 1, p], rsem.at[d - 1, p],
                right if way == "R" else left))

    def along_zh(way, d, h):
        sign = 1 if way == "R" else -1
        g = PLACE[sign * d if d < 4 else 4]
        buf, ssem, rsem = (R1, r1s, r1r) if way == "R" else (L1, l1s, l1r)
        here = M1.at[g, low[h]]
        before = ring.get((way + "h", d + 1, h))
        if before is not None:
            before.wait_recv()
            here[...] = here[...] + buf[d, h]
        if d > 0:
            ring[way + "h", d, h] = start(remote(
                here, buf.at[d - 1, h], ssem.at[d - 1, h], rsem.at[d - 1, h],
                right if way == "R" else left))

    def step_F(p):
        along_z("R", 0, p)
        along_z("L", 0, p)
        if p >= 2:
            last[p] = start(remote(
                M0.at[own, 1, low[p - 2]], FY.at[low[p - 2]], fs.at[p - 2], fr.at[p - 2],
                beside))

    def step_E(h, part):
        if h == 0:
            step_F(part)
            last[part + 2].wait_recv()
            M0[own, 0, low[part]] = M0[own, 0, low[part]] + FY[low[part]]
        else:
            along_zh("R", 0, part)
            along_zh("L", 0, part)

    def step_C(n):
        if n == 1:
            for k in range(1, 8):
                g = PLACE[k if k <= 4 else k - 8]
                sums["z", k] = start(remote(
                    MC.at[g], MZ.at[k - 1], zs.at[k - 1], zr.at[k - 1], along(k)))
        elif n == 2:
            rows4 = MC[own]
            for k in range(1, 8):
                sums["z", k].wait_recv()
                rows4 = rows4 + MZ[k - 1]
            MX[3] = rows4
            for k in range(3):
                sums["x", k] = start(remote(
                    MX.at[3], MX.at[k], xs.at[k], xr.at[k], aside(k + 1)))
        else:
            rows4 = MX[3]
            for k in range(3):
                sums["x", k].wait_recv()
                rows4 = rows4 + MX[k]
            MY[3] = rows4
            for k in range(3):
                sums["y", k] = start(remote(
                    MY.at[3], MY.at[k], us.at[k], ur.at[k], over_y[k]))

    def step_O(h):
        if h == 1:
            for k in range(3):
                sums["y", k].wait_recv()
        mean = (MY[3, h:h + 1] + MY[1, h:h + 1] + MY[0, 2 + h:3 + h]
                + MY[2, 2 + h:3 + h]) * (1.0 / 1024.0)
        block = ((M0[own, 0] if h == 0 else M1[own]) - mean) * (1.0 / BLOCK)
        TMP[pl.ds(0, 64, stride=2), :] = block[0:64]
        TMP[pl.ds(1, 64, stride=2), :] = block[64:128]
        out[h * TBLK:(h + 1) * TBLK, :] = TMP[0:QL].T

    MC[...] = jnp.zeros((8, 8, TBLK), F32)
    for name in STEPS_OF_SUM:
        kind, digits = name.rstrip("0123456789"), [int(c) for c in name if c.isdigit()]
        if kind in ("R", "L"):
            along_z(kind, *digits)
        elif kind in ("Rh", "Lh"):
            along_zh(kind[0], *digits)
        else:
            {"S": step_S, "M": step_M, "J": step_J, "F": step_F, "E": step_E,
             "C": step_C, "O": step_O}[kind](*digits)

    for copy in sent:
        copy.wait_send()


def local(query_words, lib_bits, cutoff, counts, targets, activity_tiles):
    V = pltpu.VMEM
    dma = pltpu.SemaphoreType.DMA
    block = (QL, TBLK)
    return pl.pallas_call(
        kernel,
        out_shape=pltpu.VMEM((2 * TBLK, QL), F32),
        in_specs=[pl.BlockSpec(memory_space=pl.ANY)] * 6,
        out_specs=pl.BlockSpec(memory_space=V),
        scratch_shapes=[
            V((NBITS, 2 * QL), F8),
            V((NBUF, ROWS, NBITS), BF),
            V((NBUF, ROWS // BLOCK, KMAX, BLOCK, TBLK), BF),
            V((2, ROWS, 2 * QL), F32),
            V((2, QL, ROWS), BF),
            V((SLOTS + 1,) + block, F32),
            V((4, WORDS), jnp.int32),
            V((LIB // 128, 128), F32),
            V((1, SLOTS // KMAX), jnp.int32),
            V((KMAX, SLOTS // KMAX), jnp.int32),
            V((8, 128), jnp.int32),
            pltpu.SMEM((8, 128), jnp.int32),
            V((8, 128), jnp.int32),
            V((8, 128), jnp.int32),
            V((3, 8, 128), jnp.int32),
            V((4, 8, 8, 128), jnp.int32),
            V((8, 4) + block, F32),
            V((8, 4) + block, F32),
            V((8, 2) + block, F32),
            V((8,) + block, F32),
            V((8,) + block, F32),
            V((8,) + block, F32),
            V(block, F32),
            V((4, 4, HALF, TBLK), F32),
            V((4, 4, HALF, TBLK), F32),
            V((4, 2, HALF, TBLK), F32),
            V((4, 2, HALF, TBLK), F32),
            V((8, 8, TBLK), F32),
            V((7, 8, TBLK), F32),
            V((4, 8, TBLK), F32),
            V((4, 8, TBLK), F32),
            V((QL + 8, TBLK), F32),
            dma((NBUF,)), dma((NBUF,)), dma((4,)), dma,
            dma((3,)), dma((3,)), dma((31,)), dma((31,)),
            dma((8,)), dma((8,)), dma((8, 2)), dma((8, 2)),
            dma((2,)), dma((2,)),
            dma((4, 4)), dma((4, 4)), dma((4, 4)), dma((4, 4)),
            dma((4, 2)), dma((4, 2)), dma((4, 2)), dma((4, 2)),
            dma((7,)), dma((7,)), dma((3,)), dma((3,)), dma((3,)), dma((3,)),
        ],
        compiler_params=pltpu.CompilerParams(
            collective_id=0, has_side_effects=True, vmem_limit_bytes=60 * 2**20),
        cost_estimate=pl.CostEstimate(
            flops=2 * LIB * NBITS * 2 * QL, bytes_accessed=48 * 2**20,
            transcendentals=LIB * QL),
        name="screen",
    )(query_words, cutoff.reshape(LIB // 128, 128), counts.reshape(1, SLOTS // KMAX),
      targets.T, lib_bits, activity_tiles)


def solution(mesh):
    in_specs = (
        P(("query", "lib"), None),
        P("lib", None),
        P("lib"),
        P("lib"),
        P("lib", None),
        P("lib", None, None, None),
    )
    out_specs = P("lib", "query")
    return jax.shard_map(local, mesh=mesh, in_specs=in_specs, out_specs=out_specs, check_vma=False)
```
